512 devices in a mesh: seq: 128 (over x, z, y_lo), fsdp: 4 (over y_hi, core).
Axes of the slice: x: 4, y: 4 (y_hi: 2, y_lo: 2; y = y_hi * 2 + y_lo), z: 16, core: 2. Of those that a mesh axis runs over, the one named last changes fastest.
Arguments:
- tokens: bfloat16 [16384, 1024], P('seq', 'fsdp'), may hold values from -6 to 6
- w_in: bfloat16 [1024, 3, 1024], P('fsdp'), may hold values from -0.1875 to 0.1875
- short_w: float32 [3, 3, 1024], P(None, None, 'fsdp'), may hold values from -3.5 to 3.5
- long_filter: float32 [1024, 16384], P('fsdp', 'seq'), may hold values from -1.5 to 1.5, as said below
- skip_gain: float32 [1024], P('fsdp'), may hold values from -4 to 4
- w_out: bfloat16 [1024, 1024], P(None, 'fsdp'), may hold values from -0.1875 to 0.1875
Outputs:
- result: float32 [16384, 1024], P('seq', 'fsdp')
The draws below stay inside these ranges and needn't reach their ends.
Inputs may be any that keep to these rules, and one draw needn't show every extreme that they name: `long_filter`: filter taps of each channel.
All inputs are finite; a program needn't handle non-finite values.
Results may differ from the reference program's by a relative error of at most 0.0034.
Values may be sent and summed in bfloat16 or wider, within the bound.
No kernel may reach another device: no remote copies, remote signals or barrier semaphores. Data moves between devices by JAX's collectives and lax.ppermute only.
A program may use at most 64 MiB of HBM per device.

```python
import jax
import jax.numpy as jnp

D = 1024
C = 1024
TOKENS = 16384


def decaying_taps(key_rate, key_tap, low_end, high_end):
    rate_col = jnp.exp(jax.random.uniform(key_rate, (C, 1), jnp.float32, jnp.log(low_end), jnp.log(high_end)))
    positions = jnp.arange(TOKENS, dtype=jnp.float32)[None, :]
    scale_col = jnp.sqrt(jnp.expm1(-2.0 * rate_col) / jnp.expm1(-2.0 * rate_col * TOKENS))
    taps_drawn = jnp.clip(jax.random.normal(key_tap, (C, TOKENS), jnp.float32), -6.0, 6.0)
    return taps_drawn * scale_col * jnp.exp(-rate_col * positions)


def draw_long_filter(key, part):
    key = jax.random.fold_in(key, 11)
    key_rate = jax.random.fold_in(key, 1)
    key_tap = jax.random.fold_in(key, 2)
    key_slow_rate = jax.random.fold_in(key, 3)
    key_slow_tap = jax.random.fold_in(key, 4)
    slow_share = 0.08
    low_end = 1.0 / TOKENS
    high_end = 1.0 / 32.0
    main_part = decaying_taps(key_rate, key_tap, low_end, high_end)
    slow_part = decaying_taps(key_slow_rate, key_slow_tap, 0.25 / TOKENS, 1.0 / TOKENS)
    return jnp.sqrt(1.0 - slow_share) * main_part + jnp.sqrt(slow_share) * slow_part


def shard_levels(rng, dims, cuts, smallest, top_value):
    gain = 1.0
    for dim, parts in cuts:
        draws = jax.random.uniform(jax.random.fold_in(jax.random.fold_in(rng, 6), dim), (parts,), jnp.float32, smallest / len(cuts), top_value / len(cuts))
        gain = gain * jnp.repeat(jnp.exp(draws), dims[dim] // parts).reshape((-1,) + (1,) * (len(dims) - 1 - dim))
    return gain


def normal_values(key, shape, deviation, reach, pieces=(), kind=jnp.bfloat16):
    loudness = shard_levels(key, shape, pieces, -0.22, 0.18) if pieces else 1.0
    array = jax.random.normal(key, shape, jnp.float32) * deviation * loudness
    return jnp.minimum(jnp.maximum(array, -reach), reach).astype(kind)


def setup_inputs(seed: int = 0) -> dict:
    arg_keys = jax.random.split(jax.random.key(seed), 7)
    return {
        "tokens": normal_values(arg_keys[0], (TOKENS, D), 1.0, 6.0, ((0, 128), (1, 4))),
        "w_in": normal_values(arg_keys[1], (D, 3, C), D ** -0.5, 0.1875, ((0, 4),)),
        "short_w": normal_values(arg_keys[2], (3, 3, C), 3 ** -0.5, 3.5, ((2, 4),), jnp.float32),
        "long_filter": draw_long_filter(jax.random.fold_in(arg_keys[6], 71), 0),
        "skip_gain": normal_values(arg_keys[4], (C,), 1.0, 4.0, ((0, 4),), jnp.float32),
        "w_out": normal_values(arg_keys[5], (D, C), C ** -0.5, 0.1875, ((1, 4),)),
    }


def reference(tokens, w_in, short_w, long_filter, skip_gain, w_out):
    projected = jnp.dot(tokens, w_in.reshape(D, 3 * C), preferred_element_type=jnp.float32).reshape(TOKENS, 3, C)
    extended = jnp.concatenate([jnp.zeros((2, 3, C), jnp.float32), projected], axis=0)
    mixed = short_w[0] * extended[2:] + short_w[1] * extended[1:-1] + short_w[2] * extended[:-2]
    query = mixed[:, 0]
    signal = mixed[:, 1] * mixed[:, 2]
    length = 2 * TOKENS
    spectrum = jnp.fft.rfft(signal, n=length, axis=0) * jnp.fft.rfft(long_filter.T, n=length, axis=0)
    convolved = jnp.fft.irfft(spectrum, n=length, axis=0)[:TOKENS]
    gated = (query * (convolved + skip_gain * signal)).astype(jnp.bfloat16)
    return jnp.dot(gated, w_out.T, preferred_element_type=jnp.float32)
```

```python
import jax
import jax.numpy as jnp
import numpy as np
from jax import lax
from jax.sharding import PartitionSpec as P

HIGH = lax.Precision.HIGHEST
PROJ_SCALE = 1024.0
TAP_SCALE = 32768.0


def encode(values, scale):
    root = jnp.sqrt(jnp.abs(values)) * scale
    return jnp.where(values < 0, -root, root).astype(jnp.float16)


def decode(code, scale):
    root = code.astype(jnp.float32) * (1.0 / scale)
    return root * jnp.abs(root)


def dot(left, right):
    return jnp.dot(left, right, precision=HIGH, preferred_element_type=jnp.float32)


def transform_tables(rows, cols):
    total = rows * cols
    a, b = np.arange(rows), np.arange(cols)
    first = np.exp(-2j * np.pi * np.outer(a, a) / rows - 0.5j * np.pi * a[None, :] / rows)
    twist = np.exp(-2j * np.pi * np.outer(a, b) / total - 0.5j * np.pi * b[None, :] / total)
    second = np.exp(-2j * np.pi * np.outer(b, b) / cols)
    return first, twist, second


def f32(table):
    return jnp.asarray(np.asarray(table, np.float32))


def causal_convolution(signal, taps):
    rows, channels, cols = signal.shape
    first, twist, second = transform_tables(rows, cols)
    data = jnp.concatenate([signal, taps], axis=1).reshape(rows, -1)
    spread = dot(f32(np.concatenate([first.real, first.imag])), data).reshape(2, rows, 2 * channels, cols)
    t_re, t_im = f32(twist.real)[:, None, :], f32(twist.imag)[:, None, :]
    re = spread[0] * t_re - spread[1] * t_im
    im = spread[0] * t_im + spread[1] * t_re
    forward = f32(np.block([[second.real, second.imag], [-second.imag, second.real]]))
    freq = dot(jnp.concatenate([re, im], axis=-1).reshape(-1, 2 * cols), forward)
    freq = freq.reshape(rows, 2, channels, 2, cols)
    s_re, s_im, h_re, h_im = freq[:, 0, :, 0], freq[:, 0, :, 1], freq[:, 1, :, 0], freq[:, 1, :, 1]
    both = jnp.concatenate([s_re * h_re - s_im * h_im, s_re * h_im + s_im * h_re], axis=-1)
    inverse = f32(np.block([[second.real, -second.imag], [second.imag, second.real]]))
    back = dot(both.reshape(-1, 2 * cols), inverse).reshape(rows, channels, 2, cols)
    re = back[:, :, 0] * t_re + back[:, :, 1] * t_im
    im = back[:, :, 1] * t_re - back[:, :, 0] * t_im
    last = f32(np.concatenate([first.real.T, first.imag.T], axis=1) / (rows * cols))
    stacked = jnp.concatenate([re, im], axis=0).reshape(2 * rows, -1)
    return dot(last, stacked).reshape(rows, channels, cols)


def delayed(blocks):
    carry = jnp.concatenate([jnp.zeros_like(blocks[:1, ..., -1:]), blocks[:-1, ..., -1:]], axis=0)
    return jnp.concatenate([carry, blocks[..., :-1]], axis=-1)


def on_device(tokens, w_in, short_w, long_filter, skip_gain, w_out):
    seq_count = lax.axis_size("seq")
    fsdp_count = lax.axis_size("fsdp")
    seq_index = lax.axis_index("seq")
    local_tok = tokens.shape[0]
    channels = long_filter.shape[0]
    own = channels // seq_count
    partial = jnp.einsum("dhc,td->hct", w_in, tokens, preferred_element_type=jnp.float32)
    sent = encode(partial, PROJ_SCALE).reshape(3, fsdp_count, channels, local_tok)
    parts = lax.all_to_all(sent.transpose(1, 0, 2, 3), "fsdp", 0, 0, tiled=True)
    projected = jnp.sum(decode(parts, PROJ_SCALE), axis=0)
    packed = jnp.concatenate([encode(projected, PROJ_SCALE), encode(long_filter, TAP_SCALE)[None]])
    packed = packed.reshape(4, seq_count, own, local_tok).transpose(1, 0, 2, 3)
    whole = lax.all_to_all(packed, "seq", 0, 0, tiled=True)
    now = decode(whole[:, :3], PROJ_SCALE)
    taps = decode(whole[:, 3], TAP_SCALE)
    short = lax.dynamic_slice_in_dim(short_w, seq_index * own, own, 2)[..., None]
    skip = lax.dynamic_slice_in_dim(skip_gain, seq_index * own, own, 0)[:, None]
    before = delayed(now)
    mixed = short[0] * now + short[1] * before + short[2] * delayed(before)
    query = mixed[:, 0]
    signal = mixed[:, 1] * mixed[:, 2]
    convolved = causal_convolution(signal, taps)
    gated = (query * (convolved + skip * signal)).astype(jnp.bfloat16)
    home = lax.all_to_all(gated, "seq", 0, 0, tiled=True).reshape(channels, local_tok)
    outcome = lax.dot_general(home, w_out, (((0,), (1,)), ((), ())), preferred_element_type=jnp.float32)
    outcome = outcome.reshape(local_tok, fsdp_count, -1).transpose(1, 0, 2).astype(jnp.bfloat16)
    shares = lax.all_to_all(outcome, "fsdp", 0, 0, tiled=True)
    return jnp.sum(shares.astype(jnp.float32), axis=0)


def solution(mesh):
    in_specs = (
        P("seq", "fsdp"),
        P("fsdp", None, None),
        P(None, None, "fsdp"),
        P("fsdp", "seq"),
        P("fsdp"),
        P(None, "fsdp"),
    )
    out_specs = P("seq", "fsdp")
    return jax.shard_map(
        on_device, mesh=mesh, in_specs=in_specs, out_specs=out_specs, check_vma=False
    )
```

```python
import jax
import jax.numpy as jnp
import numpy as np
from jax import lax
from jax.experimental import pallas as pl
from jax.experimental.pallas import tpu as pltpu
from jax.sharding import PartitionSpec as P

PROJ_SCALE = 2.0**21
TAP_SCALE = 2.0**31
TINY = 1e-37
VMEM = pl.BlockSpec(memory_space=pltpu.VMEM)
SMEM = pl.BlockSpec(memory_space=pltpu.SMEM)
PARAMS = pltpu.CompilerParams(vmem_limit_bytes=32 * 1024 * 1024)


def encode(scaled):
    return ((scaled * scaled) * (scaled * jnp.abs(scaled))).astype(jnp.bfloat16)


def decode(code):
    wide = code.astype(jnp.float32)
    root = lax.rsqrt(lax.rsqrt(jnp.maximum(jnp.abs(wide), TINY)))
    return jnp.where(wide < 0, -root, root)


def project_kernel(tokens_ref, w_ref, out_ref):
    peers, _, _, channels = out_ref.shape
    for peer in range(peers):
        part = jnp.dot(
            tokens_ref[...], w_ref[0, :, peer * channels : (peer + 1) * channels], preferred_element_type=jnp.float32
        )
        out_ref[peer, 0] = encode(part * PROJ_SCALE)


def project(tokens, weights, peers):
    kinds, depth, wide = weights.shape
    rows, channels = tokens.shape[0], wide // peers
    return pl.pallas_call(
        project_kernel,
        grid=(kinds,),
        in_specs=[
            pl.BlockSpec((rows, depth), lambda kind: (0, 0)),
            pl.BlockSpec((1, depth, wide), lambda kind: (kind, 0, 0)),
        ],
        out_specs=pl.BlockSpec((peers, 1, rows, channels), lambda kind: (0, kind, 0, 0)),
        out_shape=jax.ShapeDtypeStruct((peers, kinds, rows, channels), jnp.bfloat16),
        compiler_params=PARAMS,
        name="project",
    )(tokens, weights)


def pack_kernel(parts_ref, taps_ref, out_ref, flat_ref, packed_ref):
    peers, kinds, _, channels = parts_ref.shape
    half = channels // 2
    for kind in range(kinds + 1):
        if kind < kinds:
            total = decode(parts_ref[0, kind])
            for peer in range(1, peers):
                total = total + decode(parts_ref[peer, kind])
            flat_ref[...] = total.T
        else:
            flat_ref[...] = taps_ref[...] * TAP_SCALE
        for j in range(2):
            packed_ref[pl.ds(2 * kind + j, half, stride=8), :] = flat_ref[pl.ds(j, half, stride=2), :]
    out_ref[...] = encode(packed_ref[...])


def pack(parts, taps):
    channels, rows = taps.shape
    return pl.pallas_call(
        pack_kernel,
        in_specs=[VMEM, VMEM],
        out_specs=VMEM,
        out_shape=jax.ShapeDtypeStruct((4 * channels, rows), jnp.bfloat16),
        scratch_shapes=[pltpu.VMEM((channels, rows), jnp.float32), pltpu.VMEM((4 * channels, rows), jnp.float32)],
        compiler_params=PARAMS,
        name="pack",
    )(parts, taps)


def split(values):
    high = values.astype(jnp.bfloat16)
    return high, (values - high.astype(jnp.float32)).astype(jnp.bfloat16)


def dot3(left, right):
    (a, b), (c, d) = left, right
    low = jnp.dot(a, d, preferred_element_type=jnp.float32) + jnp.dot(b, c, preferred_element_type=jnp.float32)
    return jnp.dot(a, c, preferred_element_type=jnp.float32) + low


def delayed(block, by):
    rows, cols = block.shape
    moved = pltpu.roll(block, by, 1)
    col = lax.broadcasted_iota(jnp.int32, (rows, cols), 1)
    row = lax.broadcasted_iota(jnp.int32, (rows, cols), 0)
    carried = jnp.where(row == 0, 0.0, pltpu.roll(moved, 1, 0))
    return jnp.where(col < by, carried, moved)


def convolve_kernel(code_ref, short_ref, skip_ref, first_ref, twist_ref, mid_ref, inv_ref, last_ref, out_ref, now_ref, mix_ref):
    rows, cols = twist_ref.shape[1:]
    now_ref[...] = decode(code_ref[...])

    def mixed(kind, j):
        r = 2 * kind + j
        block = now_ref[pl.ds(r, rows, stride=8), :] * (1.0 / PROJ_SCALE)
        return short_ref[0, r] * block + short_ref[1, r] * delayed(block, 1) + short_ref[2, r] * delayed(block, 2)

    signal = [mixed(1, j) * mixed(2, j) for j in range(2)]
    taps = [now_ref[pl.ds(6 + j, rows, stride=8), :] * (1.0 / TAP_SCALE) for j in range(2)]
    data = jnp.concatenate(signal + taps, axis=1)
    spread = dot3((first_ref[0], first_ref[1]), split(data))
    t_re, t_im = twist_ref[0], twist_ref[1]
    turned = []
    for k in range(4):
        re = spread[:rows, k * cols : (k + 1) * cols]
        im = spread[rows:, k * cols : (k + 1) * cols]
        turned.append(jnp.concatenate([re * t_re - im * t_im, re * t_im + im * t_re], axis=1))
    freq = dot3(split(jnp.concatenate(turned, axis=0)), (mid_ref[0], mid_ref[1]))
    both = []
    for j in range(2):
        s_re, s_im = freq[j * rows : (j + 1) * rows, :cols], freq[j * rows : (j + 1) * rows, cols:]
        h_re, h_im = freq[(2 + j) * rows : (3 + j) * rows, :cols], freq[(2 + j) * rows : (3 + j) * rows, cols:]
        both.append(jnp.concatenate([s_re * h_re - s_im * h_im, s_re * h_im + s_im * h_re], axis=1))
    back = dot3(split(jnp.concatenate(both, axis=0)), (inv_ref[0], inv_ref[1]))
    real, imag = [], []
    for j in range(2):
        re, im = back[j * rows : (j + 1) * rows, :cols], back[j * rows : (j + 1) * rows, cols:]
        real.append(re * t_re + im * t_im)
        imag.append(im * t_re - re * t_im)
    stacked = jnp.concatenate([jnp.concatenate(real, axis=1), jnp.concatenate(imag, axis=1)], axis=0)
    convolved = dot3((last_ref[0], last_ref[1]), split(stacked))
    for j in range(2):
        gated = mixed(0, j) * (convolved[:, j * cols : (j + 1) * cols] + skip_ref[0, j] * signal[j])
        mix_ref[pl.ds(j, rows, stride=2), :] = gated
    out_ref[...] = mix_ref[...].astype(jnp.bfloat16)


def tables(rows, cols):
    total = rows * cols
    a, b = np.arange(rows), np.arange(cols)
    first = np.exp(-2j * np.pi * np.outer(a, a) / rows - 0.5j * np.pi * a[None, :] / rows)
    twist = np.exp(-2j * np.pi * np.outer(a, b) / total - 0.5j * np.pi * b[None, :] / total)
    second = np.exp(-2j * np.pi * np.outer(b, b) / cols)

    def halves(table):
        table = table.astype(np.float32)
        high = table.astype(jnp.bfloat16)
        return jnp.asarray(np.stack([high, (table - high.astype(np.float32)).astype(jnp.bfloat16)]))

    return (
        halves(np.concatenate([first.real, first.imag])),
        jnp.asarray(np.stack([twist.real, twist.imag]).astype(np.float32)),
        halves(np.block([[second.real, second.imag], [-second.imag, second.real]])),
        halves(np.block([[second.real, -second.imag], [second.imag, second.real]])),
        halves(np.concatenate([first.real.T, first.imag.T], axis=1) / total),
    )


def convolve(code, short, skip, rows, cols):
    return pl.pallas_call(
        convolve_kernel,
        in_specs=[VMEM, SMEM, SMEM] + [VMEM] * 5,
        out_specs=VMEM,
        out_shape=jax.ShapeDtypeStruct((2 * rows, cols), jnp.bfloat16),
        scratch_shapes=[pltpu.VMEM((8 * rows, cols), jnp.float32), pltpu.VMEM((2 * rows, cols), jnp.float32)],
        compiler_params=PARAMS,
        name="convolve",
    )(code, short, skip, *tables(rows, cols))


def output_kernel(index_ref, gated_ref, *refs):
    *w_refs, out_ref = refs
    channels = w_refs[0].shape[1]
    total = 0.0
    for step, w_ref in enumerate(w_refs):
        start = pl.multiple_of((index_ref[0] ^ step) * channels, channels)
        total = total + jnp.dot(w_ref[...], gated_ref[pl.ds(start, channels), :], preferred_element_type=jnp.float32)
    out_ref[...] = total.T


def output(index, gated, columns):
    return pl.pallas_call(
        output_kernel,
        in_specs=[SMEM, VMEM] + [VMEM] * len(columns),
        out_specs=VMEM,
        out_shape=jax.ShapeDtypeStruct((gated.shape[1], columns[0].shape[0]), jnp.float32),
        compiler_params=PARAMS,
        name="output",
    )(index, gated, *columns)


def exchanged(shares, axis):
    index = lax.axis_index(axis)
    peers = shares.shape[0]
    pieces = [lax.dynamic_index_in_dim(shares, index ^ step, 0, keepdims=False) for step in range(peers)]
    return pieces[:1] + [
        lax.ppermute(pieces[step], axis, [(i, i ^ step) for i in range(peers)]) for step in range(1, peers)
    ]


def on_device(tokens, w_in, short_w, long_filter, skip_gain, w_out):
    seq_count = lax.axis_size("seq")
    fsdp_count = lax.axis_size("fsdp")
    seq_index = lax.axis_index("seq")
    fsdp_index = lax.axis_index("fsdp")
    channels, local_tok = long_filter.shape
    partial = project(tokens, w_in.transpose(1, 0, 2), fsdp_count)
    parts = lax.all_to_all(partial, "fsdp", 0, 0, tiled=True)
    packed = pack(parts, long_filter).reshape(seq_count, -1, local_tok)
    whole = lax.all_to_all(packed, "seq", 0, 0, tiled=True).reshape(-1, local_tok)
    columns = exchanged(w_out.reshape(fsdp_count, -1, channels), "fsdp")
    short = lax.dynamic_slice_in_dim(short_w, seq_index * 2, 2, 2).reshape(3, 6)
    skip = lax.dynamic_slice_in_dim(skip_gain, seq_index * 2, 2, 0).reshape(1, 2)
    gated = convolve(whole, short, skip, seq_count, local_tok)
    home = lax.all_to_all(gated.reshape(seq_count, 2, local_tok), "seq", 0, 0, tiled=True)
    gathered = lax.all_gather(home.reshape(channels, local_tok), "fsdp", axis=0, tiled=True)
    return output(fsdp_index.reshape(1), gathered, columns)


def solution(mesh):
    in_specs = (
        P("seq", "fsdp"),
        P("fsdp", None, None),
        P(None, None, "fsdp"),
        P("fsdp", "seq"),
        P("fsdp"),
        P(None, "fsdp"),
    )
    out_specs = P("seq", "fsdp")
    return jax.shard_map(
        on_device, mesh=mesh, in_specs=in_specs, out_specs=out_specs, check_vma=False
    )
```

```python
import jax
import jax.numpy as jnp
import numpy as np
from jax import lax
from jax.experimental import pallas as pl
from jax.experimental.pallas import tpu as pltpu
from jax.sharding import PartitionSpec as P

PROJ_SCALE = 2.0**21
TAP_SCALE = 2.0**31
TINY = 1e-37
VMEM = pl.BlockSpec(memory_space=pltpu.VMEM)
SMEM = pl.BlockSpec(memory_space=pltpu.SMEM)
PARAMS = pltpu.CompilerParams(vmem_limit_bytes=32 * 1024 * 1024)


def encode(scaled):
    return ((scaled * scaled) * (scaled * jnp.abs(scaled))).astype(jnp.bfloat16)


def decode(code):
    wide = code.astype(jnp.float32)
    root = lax.rsqrt(lax.rsqrt(jnp.maximum(jnp.abs(wide), TINY)))
    return jnp.where(wide < 0, -root, root)


def project_kernel(tokens_ref, w_ref, out_ref):
    peers, _, _, channels = out_ref.shape
    for peer in range(peers):
        part = jnp.dot(
            tokens_ref[...], w_ref[0, :, peer * channels : (peer + 1) * channels], preferred_element_type=jnp.float32
        )
        out_ref[peer, 0] = encode(part)


def project(tokens, weights, peers):
    kinds, depth, wide = weights.shape
    rows, channels = tokens.shape[0], wide // peers
    return pl.pallas_call(
        project_kernel,
        grid=(kinds,),
        in_specs=[
            pl.BlockSpec((rows, depth), lambda kind: (0, 0)),
            pl.BlockSpec((1, depth, wide), lambda kind: (kind, 0, 0)),
        ],
        out_specs=pl.BlockSpec((peers, 1, rows, channels), lambda kind: (0, kind, 0, 0)),
        out_shape=jax.ShapeDtypeStruct((peers, kinds, rows, channels), jnp.bfloat16),
        compiler_params=PARAMS,
        name="project",
    )(tokens, weights)


def pack_kernel(parts_ref, taps_ref, out_ref, flat_ref, packed_ref):
    peers, kinds, _, channels = parts_ref.shape
    half = channels // 2
    for kind in range(kinds + 1):
        if kind < kinds:
            total = decode(parts_ref[0, kind])
            for peer in range(1, peers):
                total = total + decode(parts_ref[peer, kind])
            flat_ref[...] = total.T
        else:
            flat_ref[...] = taps_ref[...] * TAP_SCALE
        for j in range(2):
            packed_ref[pl.ds(2 * kind + j, half, stride=8), :] = flat_ref[pl.ds(j, half, stride=2), :]
    out_ref[...] = encode(packed_ref[...])


def pack(parts, taps):
    channels, rows = taps.shape
    return pl.pallas_call(
        pack_kernel,
        in_specs=[VMEM, VMEM],
        out_specs=VMEM,
        out_shape=jax.ShapeDtypeStruct((4 * channels, rows), jnp.bfloat16),
        scratch_shapes=[pltpu.VMEM((channels, rows), jnp.float32), pltpu.VMEM((4 * channels, rows), jnp.float32)],
        compiler_params=PARAMS,
        name="pack",
    )(parts, taps)


def split(values):
    high = values.astype(jnp.bfloat16)
    return high, (values - high.astype(jnp.float32)).astype(jnp.bfloat16)


def dot3(left, right):
    (a, b), (c, d) = left, right
    low = jnp.dot(a, d, preferred_element_type=jnp.float32) + jnp.dot(b, c, preferred_element_type=jnp.float32)
    return jnp.dot(a, c, preferred_element_type=jnp.float32) + low


def delayed(block, by):
    rows, cols = block.shape
    moved = pltpu.roll(block, by, 1)
    col = lax.broadcasted_iota(jnp.int32, (rows, cols), 1)
    row = lax.broadcasted_iota(jnp.int32, (rows, cols), 0)
    carried = jnp.where(row == 0, 0.0, pltpu.roll(moved, 1, 0))
    return jnp.where(col < by, carried, moved)


def convolve_kernel(code_ref, short_ref, skip_ref, first_ref, twist_ref, mid_ref, inv_ref, last_ref, out_ref, now_ref, mix_ref):
    rows, cols = twist_ref.shape[1:]
    now_ref[...] = decode(code_ref[...])
    shift = short_ref.shape[2] - 2 * lax.axis_index("seq")
    short = [pltpu.roll(short_ref[tap], shift, 1) for tap in range(3)]
    skip = pltpu.roll(skip_ref[...], shift, 1)

    def mixed(kind, j):
        block = now_ref[pl.ds(2 * kind + j, rows, stride=8), :] * (1.0 / PROJ_SCALE)
        weights = [short[tap][kind : kind + 1, j : j + 1] for tap in range(3)]
        return weights[0] * block + weights[1] * delayed(block, 1) + weights[2] * delayed(block, 2)

    signal = [mixed(1, j) * mixed(2, j) for j in range(2)]
    taps = [now_ref[pl.ds(6 + j, rows, stride=8), :] * (1.0 / TAP_SCALE) for j in range(2)]
    data = jnp.concatenate(signal + taps, axis=1)
    spread = dot3((first_ref[0], first_ref[1]), split(data))
    t_re, t_im = twist_ref[0], twist_ref[1]
    turned = []
    for k in range(4):
        re = spread[:rows, k * cols : (k + 1) * cols]
        im = spread[rows:, k * cols : (k + 1) * cols]
        turned.append(jnp.concatenate([re * t_re - im * t_im, re * t_im + im * t_re], axis=1))
    freq = dot3(split(jnp.concatenate(turned, axis=0)), (mid_ref[0], mid_ref[1]))
    both = []
    for j in range(2):
        s_re, s_im = freq[j * rows : (j + 1) * rows, :cols], freq[j * rows : (j + 1) * rows, cols:]
        h_re, h_im = freq[(2 + j) * rows : (3 + j) * rows, :cols], freq[(2 + j) * rows : (3 + j) * rows, cols:]
        both.append(jnp.concatenate([s_re * h_re - s_im * h_im, s_re * h_im + s_im * h_re], axis=1))
    back = dot3(split(jnp.concatenate(both, axis=0)), (inv_ref[0], inv_ref[1]))
    real, imag = [], []
    for j in range(2):
        re, im = back[j * rows : (j + 1) * rows, :cols], back[j * rows : (j + 1) * rows, cols:]
        real.append(re * t_re + im * t_im)
        imag.append(im * t_re - re * t_im)
    stacked = jnp.concatenate([jnp.concatenate(real, axis=1), jnp.concatenate(imag, axis=1)], axis=0)
    convolved = dot3((last_ref[0], last_ref[1]), split(stacked))
    for j in range(2):
        gated = mixed(0, j) * (convolved[:, j * cols : (j + 1) * cols] + skip[:, j : j + 1] * signal[j])
        mix_ref[pl.ds(j, rows, stride=2), :] = gated
    out_ref[...] = mix_ref[...].astype(jnp.bfloat16)


def tables(rows, cols):
    total = rows * cols
    a, b = np.arange(rows), np.arange(cols)
    first = np.exp(-2j * np.pi * np.outer(a, a) / rows - 0.5j * np.pi * a[None, :] / rows)
    twist = np.exp(-2j * np.pi * np.outer(a, b) / total - 0.5j * np.pi * b[None, :] / total)
    second = np.exp(-2j * np.pi * np.outer(b, b) / cols)

    def halves(table):
        table = table.astype(np.float32)
        high = table.astype(jnp.bfloat16)
        return jnp.asarray(np.stack([high, (table - high.astype(np.float32)).astype(jnp.bfloat16)]))

    return (
        halves(np.concatenate([first.real, first.imag])),
        jnp.asarray(np.stack([twist.real, twist.imag]).astype(np.float32)),
        halves(np.block([[second.real, second.imag], [-second.imag, second.real]])),
        halves(np.block([[second.real, -second.imag], [second.imag, second.real]])),
        halves(np.concatenate([first.real.T, first.imag.T], axis=1) / total),
    )


def convolve(code, short, skip, rows, cols):
    return pl.pallas_call(
        convolve_kernel,
        in_specs=[VMEM] * 8,
        out_specs=VMEM,
        out_shape=jax.ShapeDtypeStruct((2 * rows, cols), jnp.bfloat16),
        scratch_shapes=[pltpu.VMEM((8 * rows, cols), jnp.float32), pltpu.VMEM((2 * rows, cols), jnp.float32)],
        compiler_params=PARAMS,
        name="convolve",
    )(code, short, skip, *tables(rows, cols))


def output_kernel(gated_ref, *refs):
    *w_refs, out_ref = refs
    index = lax.axis_index("fsdp")
    channels = w_refs[0].shape[1]
    total = 0.0
    for step, w_ref in enumerate(w_refs):
        start = pl.multiple_of((index ^ step) * channels, channels)
        total = total + jnp.dot(w_ref[...], gated_ref[pl.ds(start, channels), :], preferred_element_type=jnp.float32)
    out_ref[...] = total.T


def output(gated, columns):
    return pl.pallas_call(
        output_kernel,
        in_specs=[VMEM] + [VMEM] * len(columns),
        out_specs=VMEM,
        out_shape=jax.ShapeDtypeStruct((gated.shape[1], columns[0].shape[0]), jnp.float32),
        compiler_params=PARAMS,
        name="output",
    )(gated, *columns)


def exchanged(shares, axis):
    index = lax.axis_index(axis)
    peers = shares.shape[0]
    pieces = [lax.dynamic_index_in_dim(shares, index ^ step, 0, keepdims=False) for step in range(peers)]
    return pieces[:1] + [
        lax.ppermute(pieces[step], axis, [(i, i ^ step) for i in range(peers)]) for step in range(1, peers)
    ]


def on_device(tokens, w_in, short_w, long_filter, skip_gain, w_out):
    seq_count = lax.axis_size("seq")
    fsdp_count = lax.axis_size("fsdp")
    channels, local_tok = long_filter.shape
    scaled = tokens * jnp.bfloat16(PROJ_SCALE)
    partial = project(scaled, w_in.transpose(1, 0, 2), fsdp_count)
    parts = lax.all_to_all(partial, "fsdp", 0, 0, tiled=True)
    packed = pack(parts, long_filter).reshape(seq_count, -1, local_tok)
    whole = lax.all_to_all(packed, "seq", 0, 0, tiled=True).reshape(-1, local_tok)
    gated = convolve(whole, short_w, skip_gain.reshape(1, -1), seq_count, local_tok)
    gated, w_out = lax.optimization_barrier((gated, w_out))
    columns = exchanged(w_out.reshape(fsdp_count, -1, channels), "fsdp")
    home = lax.all_to_all(gated.reshape(seq_count, 2, local_tok), "seq", 0, 0, tiled=True)
    gathered = lax.all_gather(home.reshape(channels, local_tok), "fsdp", axis=0, tiled=True)
    return output(gathered, columns)


def solution(mesh):
    in_specs = (
        P("seq", "fsdp"),
        P("fsdp", None, None),
        P(None, None, "fsdp"),
        P("fsdp", "seq"),
        P("fsdp"),
        P(None, "fsdp"),
    )
    out_specs = P("seq", "fsdp")
    return jax.shard_map(
        on_device, mesh=mesh, in_specs=in_specs, out_specs=out_specs, check_vma=False
    )
```

```python
import jax
import jax.numpy as jnp
import numpy as np
from jax import lax
from jax.experimental import pallas as pl
from jax.experimental.pallas import tpu as pltpu
from jax.sharding import PartitionSpec as P

PROJ_SCALE = 2.0**21
TAP_SCALE = 2.0**31
TINY = 1e-37
VMEM = pl.BlockSpec(memory_space=pltpu.VMEM)
SMEM = pl.BlockSpec(memory_space=pltpu.SMEM)
PARAMS = pltpu.CompilerParams(vmem_limit_bytes=32 * 1024 * 1024)


def encode(scaled):
    return ((scaled * scaled) * (scaled * jnp.abs(scaled))).astype(jnp.bfloat16)


def decode(code):
    wide = code.astype(jnp.float32)
    root = lax.rsqrt(lax.rsqrt(jnp.maximum(jnp.abs(wide), TINY)))
    return jnp.where(wide < 0, -root, root)


def project_kernel(tokens_ref, w_ref, query_ref, out_ref):
    peers, kinds, _, channels = out_ref.shape
    for kind in range(kinds + 1):
        for peer in range(peers):
            columns = w_ref[kind, :, peer * channels : (peer + 1) * channels]
            part = encode(jnp.dot(tokens_ref[...], columns, preferred_element_type=jnp.float32))
            if kind == 0:
                query_ref[peer] = part
            else:
                out_ref[peer, kind - 1] = part


def project(tokens, weights, peers):
    kinds, _, wide = weights.shape
    rows, channels = tokens.shape[0], wide // peers
    return pl.pallas_call(
        project_kernel,
        in_specs=[VMEM, VMEM],
        out_specs=[VMEM, VMEM],
        out_shape=[
            jax.ShapeDtypeStruct((peers, rows, channels), jnp.bfloat16),
            jax.ShapeDtypeStruct((peers, kinds - 1, rows, channels), jnp.bfloat16),
        ],
        compiler_params=PARAMS,
        name="project",
    )(tokens, weights)


def pack_kernel(parts_ref, taps_ref, out_ref, flat_ref, packed_ref):
    peers, kinds, _, channels = parts_ref.shape
    half = channels // 2
    for kind in range(kinds + 1):
        if kind < kinds:
            total = decode(parts_ref[0, kind])
            for peer in range(1, peers):
                total = total + decode(parts_ref[peer, kind])
            flat_ref[...] = total.T
        else:
            flat_ref[...] = taps_ref[...] * TAP_SCALE
        for j in range(2):
            packed_ref[pl.ds(2 * kind + j, half, stride=8), :] = flat_ref[pl.ds(j, half, stride=2), :]
    for j in range(2 * kinds + 2, 8):
        packed_ref[pl.ds(j, half, stride=8), :] = jnp.zeros((half, packed_ref.shape[1]), jnp.float32)
    out_ref[...] = encode(packed_ref[...])


def pack(parts, taps):
    channels, rows = taps.shape
    return pl.pallas_call(
        pack_kernel,
        in_specs=[VMEM, VMEM],
        out_specs=VMEM,
        out_shape=jax.ShapeDtypeStruct((4 * channels, rows), jnp.bfloat16),
        scratch_shapes=[pltpu.VMEM((channels, rows), jnp.float32), pltpu.VMEM((4 * channels, rows), jnp.float32)],
        compiler_params=PARAMS,
        name="pack",
    )(parts, taps)


def split(values):
    high = values.astype(jnp.bfloat16)
    return high, (values - high.astype(jnp.float32)).astype(jnp.bfloat16)


def dot3(left, right):
    (a, b), (c, d) = left, right
    low = jnp.dot(a, d, preferred_element_type=jnp.float32) + jnp.dot(b, c, preferred_element_type=jnp.float32)
    return jnp.dot(a, c, preferred_element_type=jnp.float32) + low


def delayed(block, by):
    rows, cols = block.shape
    moved = pltpu.roll(block, by, 1)
    col = lax.broadcasted_iota(jnp.int32, (rows, cols), 1)
    row = lax.broadcasted_iota(jnp.int32, (rows, cols), 0)
    carried = jnp.where(row == 0, 0.0, pltpu.roll(moved, 1, 0))
    return jnp.where(col < by, carried, moved)


def convolve_kernel(code_ref, short_ref, skip_ref, first_ref, twist_ref, mid_ref, inv_ref, last_ref, out_ref, now_ref, mix_ref):
    rows, cols = twist_ref.shape[1:]
    now_ref[...] = decode(code_ref[...])
    shift = short_ref.shape[2] - 2 * lax.axis_index("seq")
    short = [pltpu.roll(short_ref[tap], shift, 1) for tap in range(3)]
    skip = pltpu.roll(skip_ref[...], shift, 1)

    def mixed(kind, j):
        block = now_ref[pl.ds(2 * kind + j, rows, stride=8), :] * (1.0 / PROJ_SCALE)
        weights = [short[tap][kind + 1 : kind + 2, j : j + 1] for tap in range(3)]
        return weights[0] * block + weights[1] * delayed(block, 1) + weights[2] * delayed(block, 2)

    signal = [mixed(0, j) * mixed(1, j) for j in range(2)]
    taps = [now_ref[pl.ds(4 + j, rows, stride=8), :] * (1.0 / TAP_SCALE) for j in range(2)]
    data = jnp.concatenate(signal + taps, axis=1)
    spread = dot3((first_ref[0], first_ref[1]), split(data))
    t_re, t_im = twist_ref[0], twist_ref[1]
    turned = []
    for k in range(4):
        re = spread[:rows, k * cols : (k + 1) * cols]
        im = spread[rows:, k * cols : (k + 1) * cols]
        turned.append(jnp.concatenate([re * t_re - im * t_im, re * t_im + im * t_re], axis=1))
    freq = dot3(split(jnp.concatenate(turned, axis=0)), (mid_ref[0], mid_ref[1]))
    both = []
    for j in range(2):
        s_re, s_im = freq[j * rows : (j + 1) * rows, :cols], freq[j * rows : (j + 1) * rows, cols:]
        h_re, h_im = freq[(2 + j) * rows : (3 + j) * rows, :cols], freq[(2 + j) * rows : (3 + j) * rows, cols:]
        both.append(jnp.concatenate([s_re * h_re - s_im * h_im, s_re * h_im + s_im * h_re], axis=1))
    back = dot3(split(jnp.concatenate(both, axis=0)), (inv_ref[0], inv_ref[1]))
    real, imag = [], []
    for j in range(2):
        re, im = back[j * rows : (j + 1) * rows, :cols], back[j * rows : (j + 1) * rows, cols:]
        real.append(re * t_re + im * t_im)
        imag.append(im * t_re - re * t_im)
    stacked = jnp.concatenate([jnp.concatenate(real, axis=1), jnp.concatenate(imag, axis=1)], axis=0)
    convolved = dot3((last_ref[0], last_ref[1]), split(stacked))
    for j in range(2):
        mix_ref[pl.ds(j, rows, stride=2), :] = convolved[:, j * cols : (j + 1) * cols] + skip[:, j : j + 1] * signal[j]
    out_ref[...] = (mix_ref[...] * jnp.abs(mix_ref[...])).astype(jnp.bfloat16)


def tables(rows, cols):
    total = rows * cols
    a, b = np.arange(rows), np.arange(cols)
    first = np.exp(-2j * np.pi * np.outer(a, a) / rows - 0.5j * np.pi * a[None, :] / rows)
    twist = np.exp(-2j * np.pi * np.outer(a, b) / total - 0.5j * np.pi * b[None, :] / total)
    second = np.exp(-2j * np.pi * np.outer(b, b) / cols)

    def halves(table):
        table = table.astype(np.float32)
        high = table.astype(jnp.bfloat16)
        return jnp.asarray(np.stack([high, (table - high.astype(np.float32)).astype(jnp.bfloat16)]))

    return (
        halves(np.concatenate([first.real, first.imag])),
        jnp.asarray(np.stack([twist.real, twist.imag]).astype(np.float32)),
        halves(np.block([[second.real, second.imag], [-second.imag, second.real]])),
        halves(np.block([[second.real, -second.imag], [second.imag, second.real]])),
        halves(np.concatenate([first.real.T, first.imag.T], axis=1) / total),
    )


def convolve(code, short, skip, rows, cols):
    return pl.pallas_call(
        convolve_kernel,
        in_specs=[VMEM] * 8,
        out_specs=VMEM,
        out_shape=jax.ShapeDtypeStruct((2 * rows, cols), jnp.bfloat16),
        scratch_shapes=[pltpu.VMEM((8 * rows, cols), jnp.float32), pltpu.VMEM((2 * rows, cols), jnp.float32)],
        compiler_params=PARAMS,
        name="convolve",
    )(code, short, skip, *tables(rows, cols))


def sum_query_kernel(*refs):
    *piece_refs, out_ref, edge_ref = refs
    rows = out_ref.shape[0]
    total = decode(piece_refs[0][:rows])
    for piece_ref in piece_refs[1:]:
        total = total + decode(piece_ref[:rows])
    out_ref[...] = total * (1.0 / PROJ_SCALE)
    edge_ref[...] = out_ref[rows - 8 :]


def sum_query(pieces, rows):
    channels = pieces[0].shape[1]
    return pl.pallas_call(
        sum_query_kernel,
        in_specs=[VMEM] * len(pieces),
        out_specs=[VMEM, VMEM],
        out_shape=[
            jax.ShapeDtypeStruct((rows, channels), jnp.float32),
            jax.ShapeDtypeStruct((8, channels), jnp.float32),
        ],
        compiler_params=PARAMS,
        name="sum_query",
    )(*pieces)


def mix_query_kernel(edge_ref, query_ref, short_ref, out_ref):
    rows = query_ref.shape[0]
    wide = jnp.concatenate([edge_ref[...], query_ref[...]], axis=0)
    total = short_ref[0, 0:1] * query_ref[...]
    for tap in range(1, 3):
        total = total + short_ref[tap, 0:1] * pltpu.roll(wide, tap, 0)[8 : 8 + rows]
    out_ref[...] = total.T


def mix_query(edge, query, short):
    return pl.pallas_call(
        mix_query_kernel,
        in_specs=[VMEM] * 3,
        out_specs=VMEM,
        out_shape=jax.ShapeDtypeStruct(query.shape[::-1], jnp.float32),
        compiler_params=PARAMS,
        name="mix_query",
    )(edge, query, short)


def gate_kernel(code_ref, query_ref, out_ref):
    wide = code_ref[...].astype(jnp.float32)
    out_ref[...] = (query_ref[...] * (wide * lax.rsqrt(jnp.maximum(jnp.abs(wide), TINY)))).astype(jnp.bfloat16)


def gate(code, query):
    return pl.pallas_call(
        gate_kernel,
        in_specs=[VMEM] * 2,
        out_specs=VMEM,
        out_shape=jax.ShapeDtypeStruct(query.shape, jnp.bfloat16),
        compiler_params=PARAMS,
        name="gate",
    )(code, query)


def output_kernel(gated_ref, *refs):
    *w_refs, out_ref = refs
    index = lax.axis_index("fsdp")
    features, channels = out_ref.shape[1], w_refs[0].shape[1]
    total = 0.0
    for step, w_ref in enumerate(w_refs):
        start = pl.multiple_of((index ^ step) * channels, channels)
        total = total + jnp.dot(w_ref[w_ref.shape[0] - features :], gated_ref[pl.ds(start, channels), :], preferred_element_type=jnp.float32)
    out_ref[...] = total.T


def output(gated, pieces, features):
    return pl.pallas_call(
        output_kernel,
        in_specs=[VMEM] + [VMEM] * len(pieces),
        out_specs=VMEM,
        out_shape=jax.ShapeDtypeStruct((gated.shape[1], features), jnp.float32),
        compiler_params=PARAMS,
        name="output",
    )(gated, *pieces)


def exchanged(piece, axis, step):
    return lax.ppermute(piece, axis, [(i, i ^ step) for i in range(lax.axis_size(axis))])


def on_device(tokens, w_in, short_w, long_filter, skip_gain, w_out):
    seq_count = lax.axis_size("seq")
    fsdp_count = lax.axis_size("fsdp")
    channels, local_tok = long_filter.shape
    scaled = tokens * jnp.bfloat16(PROJ_SCALE)
    query_parts, partial = project(scaled, w_in.transpose(1, 0, 2), fsdp_count)
    parts = lax.all_to_all(partial, "fsdp", 0, 0, tiled=True)
    parts, query_parts, w_out = lax.optimization_barrier((parts, query_parts, w_out))
    features = w_out.shape[0] // fsdp_count
    fsdp_index = lax.axis_index("fsdp")
    shares = [lax.dynamic_index_in_dim(query_parts, fsdp_index ^ step, 0, keepdims=False) for step in range(4)]
    rows = [lax.dynamic_slice_in_dim(w_out, (fsdp_index ^ step) * features, features, 0) for step in range(4)]
    pieces = [shares[0], exchanged(jnp.concatenate([shares[1], rows[1]], axis=0), "fsdp", 1)]
    pieces += [exchanged(shares[step], "fsdp", step) for step in range(2, 4)]
    packed = pack(parts, long_filter).reshape(seq_count, -1, local_tok)
    whole = lax.all_to_all(packed, "seq", 0, 0, tiled=True).reshape(-1, local_tok)
    coded = convolve(whole, short_w, skip_gain.reshape(1, -1), seq_count, local_tok)
    coded, pieces, rows = lax.optimization_barrier((coded, pieces, rows))
    query, edge = sum_query(pieces, local_tok)
    edge = lax.ppermute(edge, "seq", [(i, i + 1) for i in range(seq_count - 1)])
    query = mix_query(edge, query, short_w)
    columns = [rows[0], pieces[1]] + [exchanged(rows[step], "fsdp", step) for step in range(2, 4)]
    home = lax.all_to_all(coded.reshape(seq_count, 2, local_tok), "seq", 0, 0, tiled=True)
    gated = gate(home.reshape(channels, local_tok), query)
    gathered = lax.all_gather(gated, "fsdp", axis=0, tiled=True)
    return output(gathered, columns, features)


def solution(mesh):
    in_specs = (
        P("seq", "fsdp"),
        P("fsdp", None, None),
        P(None, None, "fsdp"),
        P("fsdp", "seq"),
        P("fsdp"),
        P(None, "fsdp"),
    )
    out_specs = P("seq", "fsdp")
    return jax.shard_map(
        on_device, mesh=mesh, in_specs=in_specs, out_specs=out_specs, check_vma=False
    )
```

```python
import functools

import jax
import jax.numpy as jnp
import numpy as np
from jax import lax
from jax.experimental import pallas as pl
from jax.experimental.pallas import tpu as pltpu
from jax.sharding import PartitionSpec as P

PROJ_SCALE = 2.0**21
TAP_SCALE = 2.0**31
TINY = 1e-37
VMEM = pl.BlockSpec(memory_space=pltpu.VMEM)
SMEM = pl.BlockSpec(memory_space=pltpu.SMEM)
PARAMS = pltpu.CompilerParams(vmem_limit_bytes=32 * 1024 * 1024)


def encode(scaled):
    return ((scaled * scaled) * (scaled * jnp.abs(scaled))).astype(jnp.bfloat16)


def decode(code):
    wide = code.astype(jnp.float32)
    root = lax.rsqrt(lax.rsqrt(jnp.maximum(jnp.abs(wide), TINY)))
    return jnp.where(wide < 0, -root, root)


def project_kernel(first, tokens_hbm, w_hbm, out_ref, tokens_ref, w_ref, sems):
    peers, kinds, _, channels = out_ref.shape
    parts = (sems.shape[0] - 1) // kinds
    depth = w_ref.shape[1] // parts

    def piece(kind, part):
        cut = pl.ds(part * depth, depth)
        return pltpu.make_async_copy(w_hbm.at[first + kind, cut], w_ref.at[kind, cut], sems.at[kind * parts + part])

    tokens_copy = pltpu.make_async_copy(tokens_hbm, tokens_ref, sems.at[kinds * parts])
    tokens_copy.start()
    for kind in range(kinds):
        for part in range(parts):
            piece(kind, part).start()
    tokens_copy.wait()
    scaled = tokens_ref[...] * jnp.bfloat16(PROJ_SCALE)
    for kind in range(kinds):
        for part in range(parts):
            piece(kind, part).wait()
        for peer in range(peers):
            columns = w_ref[kind, :, peer * channels : (peer + 1) * channels]
            out_ref[peer, kind] = encode(jnp.dot(scaled, columns, preferred_element_type=jnp.float32))


def project(tokens, weights, first, kinds, peers):
    _, depth, wide = weights.shape
    rows, channels = tokens.shape[0], wide // peers
    return pl.pallas_call(
        functools.partial(project_kernel, first),
        in_specs=[pl.BlockSpec(memory_space=pltpu.HBM)] * 2,
        out_specs=VMEM,
        out_shape=jax.ShapeDtypeStruct((peers, kinds, rows, channels), jnp.bfloat16),
        scratch_shapes=[
            pltpu.VMEM(tokens.shape, tokens.dtype),
            pltpu.VMEM((kinds, depth, wide), weights.dtype),
            pltpu.SemaphoreType.DMA((4 * kinds + 1,)),
        ],
        compiler_params=PARAMS,
        name="project",
    )(pltpu.with_memory_space_constraint(tokens, pltpu.HBM), pltpu.with_memory_space_constraint(weights, pltpu.HBM))


def project_query_kernel(tokens_ref, w_ref, w_out_ref, own_ref, bundle_ref):
    peers, rows, channels = own_ref.shape
    features = w_out_ref.shape[0] // peers
    mate = 1 - lax.rem(lax.axis_index("fsdp"), 2)
    scaled = tokens_ref[...] * jnp.bfloat16(PROJ_SCALE)
    for peer in range(peers):
        columns = w_ref[0, :, peer * channels : (peer + 1) * channels]
        own_ref[peer] = encode(jnp.dot(scaled, columns, preferred_element_type=jnp.float32))
    for chip in range(peers // 2):
        start = pl.multiple_of((2 * chip + mate) * features, features)
        bundle_ref[chip * rows : (chip + 1) * rows] = own_ref[2 * chip + mate]
        bundle_ref[2 * rows + chip * features : 2 * rows + (chip + 1) * features] = w_out_ref[pl.ds(start, features), :]


def project_query(tokens, weights, w_out, peers):
    rows, channels = tokens.shape[0], weights.shape[2] // peers
    return pl.pallas_call(
        project_query_kernel,
        in_specs=[VMEM] * 3,
        out_specs=[VMEM] * 2,
        out_shape=[
            jax.ShapeDtypeStruct((peers, rows, channels), jnp.bfloat16),
            jax.ShapeDtypeStruct((2 * rows + w_out.shape[0] // 2, channels), jnp.bfloat16),
        ],
        compiler_params=PARAMS,
        name="project_query",
    )(tokens, weights, w_out)


def pack_kernel(parts_ref, taps_ref, out_ref, flat_ref, packed_ref):
    peers, kinds, _, channels = parts_ref.shape
    half, chunk = channels // 2, 2 * kinds + 2
    for kind in range(kinds + 1):
        if kind < kinds:
            total = decode(parts_ref[0, kind])
            for peer in range(1, peers):
                total = total + decode(parts_ref[peer, kind])
            flat_ref[...] = total.T
        else:
            flat_ref[...] = taps_ref[...] * TAP_SCALE
        for j in range(2):
            packed_ref[pl.ds(2 * kind + j, half, stride=chunk), :] = flat_ref[pl.ds(j, half, stride=2), :]
    out_ref[...] = encode(packed_ref[...])


def pack(parts, taps):
    channels, rows = taps.shape
    kinds = parts.shape[1] + 1
    return pl.pallas_call(
        pack_kernel,
        in_specs=[VMEM, VMEM],
        out_specs=VMEM,
        out_shape=jax.ShapeDtypeStruct((kinds * channels, rows), jnp.bfloat16),
        scratch_shapes=[
            pltpu.VMEM((channels, rows), jnp.float32),
            pltpu.VMEM((kinds * channels, rows), jnp.float32),
        ],
        compiler_params=PARAMS,
        name="pack",
    )(parts, taps)


def split(values):
    high = values.astype(jnp.bfloat16)
    return high, (values - high.astype(jnp.float32)).astype(jnp.bfloat16)


def dot3(left, right):
    (a, b), (c, d) = left, right
    low = jnp.dot(a, d, preferred_element_type=jnp.float32) + jnp.dot(b, c, preferred_element_type=jnp.float32)
    return jnp.dot(a, c, preferred_element_type=jnp.float32) + low


def delayed(block, by):
    rows, cols = block.shape
    moved = pltpu.roll(block, by, 1)
    col = lax.broadcasted_iota(jnp.int32, (rows, cols), 1)
    row = lax.broadcasted_iota(jnp.int32, (rows, cols), 0)
    carried = jnp.where(row == 0, 0.0, pltpu.roll(moved, 1, 0))
    return jnp.where(col < by, carried, moved)


def convolve_kernel(code_ref, short_ref, skip_ref, first_ref, twist_ref, mid_ref, inv_ref, last_ref, out_ref, now_ref, mix_ref):
    rows, cols = twist_ref.shape[1:]
    now_ref[...] = decode(code_ref[...])
    shift = short_ref.shape[2] - 2 * lax.axis_index("seq")
    short = [pltpu.roll(short_ref[tap], shift, 1) for tap in range(3)]
    skip = pltpu.roll(skip_ref[...], shift, 1)

    def mixed(kind, j):
        block = now_ref[pl.ds(2 * kind + j, rows, stride=6), :] * (1.0 / PROJ_SCALE)
        weights = [short[tap][kind + 1 : kind + 2, j : j + 1] for tap in range(3)]
        return weights[0] * block + weights[1] * delayed(block, 1) + weights[2] * delayed(block, 2)

    signal = [mixed(0, j) * mixed(1, j) for j in range(2)]
    taps = [now_ref[pl.ds(4 + j, rows, stride=6), :] * (1.0 / TAP_SCALE) for j in range(2)]
    data = jnp.concatenate(signal + taps, axis=1)
    spread = dot3((first_ref[0], first_ref[1]), split(data))
    t_re, t_im = twist_ref[0], twist_ref[1]
    turned = []
    for k in range(4):
        re = spread[:rows, k * cols : (k + 1) * cols]
        im = spread[rows:, k * cols : (k + 1) * cols]
        turned.append(jnp.concatenate([re * t_re - im * t_im, re * t_im + im * t_re], axis=1))
    freq = dot3(split(jnp.concatenate(turned, axis=0)), (mid_ref[0], mid_ref[1]))
    both = []
    for j in range(2):
        s_re, s_im = freq[j * rows : (j + 1) * rows, :cols], freq[j * rows : (j + 1) * rows, cols:]
        h_re, h_im = freq[(2 + j) * rows : (3 + j) * rows, :cols], freq[(2 + j) * rows : (3 + j) * rows, cols:]
        both.append(jnp.concatenate([s_re * h_re - s_im * h_im, s_re * h_im + s_im * h_re], axis=1))
    back = dot3(split(jnp.concatenate(both, axis=0)), (inv_ref[0], inv_ref[1]))
    real, imag = [], []
    for j in range(2):
        re, im = back[j * rows : (j + 1) * rows, :cols], back[j * rows : (j + 1) * rows, cols:]
        real.append(re * t_re + im * t_im)
        imag.append(im * t_re - re * t_im)
    stacked = jnp.concatenate([jnp.concatenate(real, axis=1), jnp.concatenate(imag, axis=1)], axis=0)
    convolved = dot3((last_ref[0], last_ref[1]), split(stacked))
    for j in range(2):
        mix_ref[pl.ds(j, rows, stride=2), :] = convolved[:, j * cols : (j + 1) * cols] + skip[:, j : j + 1] * signal[j]
    out_ref[...] = (mix_ref[...] * jnp.abs(mix_ref[...])).astype(jnp.bfloat16)


def tables(rows, cols):
    total = rows * cols
    a, b = np.arange(rows), np.arange(cols)
    first = np.exp(-2j * np.pi * np.outer(a, a) / rows - 0.5j * np.pi * a[None, :] / rows)
    twist = np.exp(-2j * np.pi * np.outer(a, b) / total - 0.5j * np.pi * b[None, :] / total)
    second = np.exp(-2j * np.pi * np.outer(b, b) / cols)

    def halves(table):
        table = table.astype(np.float32)
        high = table.astype(jnp.bfloat16)
        return jnp.asarray(np.stack([high, (table - high.astype(np.float32)).astype(jnp.bfloat16)]))

    return (
        halves(np.concatenate([first.real, first.imag])),
        jnp.asarray(np.stack([twist.real, twist.imag]).astype(np.float32)),
        halves(np.block([[second.real, second.imag], [-second.imag, second.real]])),
        halves(np.block([[second.real, -second.imag], [second.imag, second.real]])),
        halves(np.concatenate([first.real.T, first.imag.T], axis=1) / total),
    )


def convolve(code, short, skip, rows, cols):
    return pl.pallas_call(
        convolve_kernel,
        in_specs=[VMEM] * 8,
        out_specs=VMEM,
        out_shape=jax.ShapeDtypeStruct((2 * rows, cols), jnp.bfloat16),
        scratch_shapes=[pltpu.VMEM((6 * rows, cols), jnp.float32), pltpu.VMEM((2 * rows, cols), jnp.float32)],
        compiler_params=PARAMS,
        name="convolve",
    )(code, short, skip, *tables(rows, cols))


def pair_query_kernel(own_ref, from_mate_ref, keep_ref, send_ref):
    index = lax.axis_index("fsdp")
    rows = keep_ref.shape[0]

    def total(peer):
        start = pl.multiple_of(lax.div(peer, 2) * rows, rows)
        return decode(own_ref[peer]) + decode(from_mate_ref[pl.ds(start, rows), :])

    keep_ref[...] = total(index)
    send_ref[...] = encode(total(index ^ 2))


def pair_query(own, from_mate):
    _, rows, channels = own.shape
    return pl.pallas_call(
        pair_query_kernel,
        in_specs=[VMEM, VMEM],
        out_specs=[VMEM, VMEM],
        out_shape=[
            jax.ShapeDtypeStruct((rows, channels), jnp.float32),
            jax.ShapeDtypeStruct((rows, channels), jnp.bfloat16),
        ],
        compiler_params=PARAMS,
        name="pair_query",
    )(own, from_mate)


def sum_query_kernel(keep_ref, code_ref, w_out_ref, from_mate_ref, out_ref, edge_ref, far_ref):
    rows, features = out_ref.shape[0], far_ref.shape[0] // 2
    index = lax.axis_index("fsdp")
    out_ref[...] = (keep_ref[...] + decode(code_ref[...])) * (1.0 / PROJ_SCALE)
    edge_ref[...] = out_ref[rows - 8 :]
    start = pl.multiple_of((index ^ 2) * features, features)
    far_ref[:features] = w_out_ref[pl.ds(start, features), :]
    start = pl.multiple_of(2 * rows + (1 - lax.div(index, 2)) * features, features)
    far_ref[features:] = from_mate_ref[pl.ds(start, features), :]


def sum_query(keep, code, w_out, from_mate):
    rows, channels = keep.shape
    return pl.pallas_call(
        sum_query_kernel,
        in_specs=[VMEM] * 4,
        out_specs=[VMEM] * 3,
        out_shape=[
            jax.ShapeDtypeStruct((rows, channels), jnp.float32),
            jax.ShapeDtypeStruct((8, channels), jnp.float32),
            jax.ShapeDtypeStruct((w_out.shape[0] // 2, channels), jnp.bfloat16),
        ],
        compiler_params=PARAMS,
        name="sum_query",
    )(keep, code, w_out, from_mate)


def mix_query_kernel(edge_ref, query_ref, short_ref, out_ref):
    rows = query_ref.shape[0]
    wide = jnp.concatenate([edge_ref[...], query_ref[...]], axis=0)
    total = short_ref[0, 0:1] * query_ref[...]
    for tap in range(1, 3):
        total = total + short_ref[tap, 0:1] * pltpu.roll(wide, tap, 0)[8 : 8 + rows]
    out_ref[...] = total.T


def mix_query(edge, query, short):
    return pl.pallas_call(
        mix_query_kernel,
        in_specs=[VMEM] * 3,
        out_specs=VMEM,
        out_shape=jax.ShapeDtypeStruct(query.shape[::-1], jnp.float32),
        compiler_params=PARAMS,
        name="mix_query",
    )(edge, query, short)


def gate_kernel(code_ref, query_ref, out_ref):
    wide = code_ref[...].astype(jnp.float32)
    out_ref[...] = (query_ref[...] * (wide * lax.rsqrt(jnp.maximum(jnp.abs(wide), TINY)))).astype(jnp.bfloat16)


def gate(code, query):
    return pl.pallas_call(
        gate_kernel,
        in_specs=[VMEM] * 2,
        out_specs=VMEM,
        out_shape=jax.ShapeDtypeStruct(query.shape, jnp.bfloat16),
        compiler_params=PARAMS,
        name="gate",
    )(code, query)


def output_kernel(gated_ref, w_out_ref, from_mate_ref, far_ref, out_ref):
    index = lax.axis_index("fsdp")
    rows, features = out_ref.shape
    channels = gated_ref.shape[0] // 4
    own = pl.multiple_of(index * features, features)
    mate = pl.multiple_of(2 * rows + lax.div(index, 2) * features, features)
    columns = [
        w_out_ref[pl.ds(own, features), :],
        from_mate_ref[pl.ds(mate, features), :],
        far_ref[:features],
        far_ref[features:],
    ]
    total = 0.0
    for step, column in enumerate(columns):
        start = pl.multiple_of((index ^ step) * channels, channels)
        total = total + jnp.dot(column, gated_ref[pl.ds(start, channels), :], preferred_element_type=jnp.float32)
    out_ref[...] = total.T


def output(gated, w_out, from_mate, far):
    return pl.pallas_call(
        output_kernel,
        in_specs=[VMEM] * 4,
        out_specs=VMEM,
        out_shape=jax.ShapeDtypeStruct((gated.shape[1], far.shape[0] // 2), jnp.float32),
        compiler_params=PARAMS,
        name="output",
    )(gated, w_out, from_mate, far)


def exchanged(piece, axis, step):
    return lax.ppermute(piece, axis, [(i, i ^ step) for i in range(lax.axis_size(axis))])


def on_device(tokens, w_in, short_w, long_filter, skip_gain, w_out):
    seq_count = lax.axis_size("seq")
    fsdp_count = lax.axis_size("fsdp")
    channels, local_tok = long_filter.shape
    weights = w_in.transpose(1, 0, 2)
    partial = project(tokens, weights, 1, 2, fsdp_count)
    parts = lax.all_to_all(partial, "fsdp", 0, 0, tiled=True)
    parts, tokens, w_out = lax.optimization_barrier((parts, tokens, w_out))
    query_parts, bundle = project_query(tokens, weights, w_out, fsdp_count)
    from_mate = exchanged(bundle, "fsdp", 1)
    keep, send = pair_query(query_parts, from_mate)
    other_chip = exchanged(send, "fsdp", 2)
    packed = pack(parts, long_filter).reshape(seq_count, 3, 2, local_tok).transpose(0, 2, 1, 3)
    whole = lax.all_to_all(packed.reshape(seq_count, 2, -1), "seq", 0, 0, tiled=True)
    whole = whole.reshape(seq_count, 2, 3, local_tok).transpose(0, 2, 1, 3).reshape(-1, local_tok)
    coded = convolve(whole, short_w, skip_gain.reshape(1, -1), seq_count, local_tok)
    coded, other_chip, from_mate = lax.optimization_barrier((coded, other_chip, from_mate))
    query, edge, far = sum_query(keep, other_chip, w_out, from_mate)
    edge = lax.ppermute(edge, "seq", [(i, i + 1) for i in range(seq_count - 1)])
    query = mix_query(edge, query, short_w)
    far = exchanged(far, "fsdp", 2)
    home = lax.all_to_all(coded.reshape(seq_count, 2, local_tok), "seq", 0, 0, tiled=True)
    gated = gate(home.reshape(channels, local_tok), query)
    gathered = lax.all_gather(gated, "fsdp", axis=0, tiled=True)
    return output(gathered, w_out, from_mate, far)


def solution(mesh):
    in_specs = (
        P("seq", "fsdp"),
        P("fsdp", None, None),
        P(None, None, "fsdp"),
        P("fsdp", "seq"),
        P("fsdp"),
        P(None, "fsdp"),
    )
    out_specs = P("seq", "fsdp")
    return jax.shard_map(
        on_device, mesh=mesh, in_specs=in_specs, out_specs=out_specs, check_vma=False
    )
```

```python
import functools

import jax
import jax.numpy as jnp
import numpy as np
from jax import lax
from jax.experimental import pallas as pl
from jax.experimental.pallas import tpu as pltpu
from jax.sharding import PartitionSpec as P

PROJ_SCALE = 2.0**21
TAP_SCALE = 2.0**31
TINY = 1e-37
VMEM = pl.BlockSpec(memory_space=pltpu.VMEM)
SMEM = pl.BlockSpec(memory_space=pltpu.SMEM)
PARAMS = pltpu.CompilerParams(vmem_limit_bytes=32 * 1024 * 1024)


def encode(scaled):
    return ((scaled * scaled) * (scaled * jnp.abs(scaled))).astype(jnp.bfloat16)


def decode(code):
    wide = code.astype(jnp.float32)
    root = lax.rsqrt(lax.rsqrt(jnp.maximum(jnp.abs(wide), TINY)))
    return jnp.where(wide < 0, -root, root)


def project_kernel(first, tokens_hbm, w_hbm, out_ref, tokens_ref, w_ref, sems):
    peers, kinds, _, channels = out_ref.shape
    parts = (sems.shape[0] - 1) // kinds
    depth = w_ref.shape[1] // parts

    def piece(kind, part):
        cut = pl.ds(part * depth, depth)
        return pltpu.make_async_copy(w_hbm.at[first + kind, cut], w_ref.at[kind, cut], sems.at[kind * parts + part])

    tokens_copy = pltpu.make_async_copy(tokens_hbm, tokens_ref, sems.at[kinds * parts])
    tokens_copy.start()
    for kind in range(kinds):
        for part in range(parts):
            piece(kind, part).start()
    tokens_copy.wait()
    scaled = tokens_ref[...] * jnp.bfloat16(PROJ_SCALE)
    for kind in range(kinds):
        for part in range(parts):
            piece(kind, part).wait()
        for peer in range(peers):
            columns = w_ref[kind, :, peer * channels : (peer + 1) * channels]
            out_ref[peer, kind] = encode(jnp.dot(scaled, columns, preferred_element_type=jnp.float32))


def project(tokens, weights, first, kinds, peers):
    _, depth, wide = weights.shape
    rows, channels = tokens.shape[0], wide // peers
    return pl.pallas_call(
        functools.partial(project_kernel, first),
        in_specs=[pl.BlockSpec(memory_space=pltpu.HBM)] * 2,
        out_specs=VMEM,
        out_shape=jax.ShapeDtypeStruct((peers, kinds, rows, channels), jnp.bfloat16),
        scratch_shapes=[
            pltpu.VMEM(tokens.shape, tokens.dtype),
            pltpu.VMEM((kinds, depth, wide), weights.dtype),
            pltpu.SemaphoreType.DMA((kinds + 1,)),
        ],
        compiler_params=PARAMS,
        name="project",
    )(pltpu.with_memory_space_constraint(tokens, pltpu.HBM), pltpu.with_memory_space_constraint(weights, pltpu.HBM))


def project_query_kernel(tokens_ref, w_ref, w_out_ref, own_ref, bundle_ref):
    peers, rows, channels = own_ref.shape
    features = w_out_ref.shape[0] // peers
    mate = 1 - lax.rem(lax.axis_index("fsdp"), 2)
    scaled = tokens_ref[...] * jnp.bfloat16(PROJ_SCALE)
    for peer in range(peers):
        columns = w_ref[0, :, peer * channels : (peer + 1) * channels]
        own_ref[peer] = encode(jnp.dot(scaled, columns, preferred_element_type=jnp.float32))
    for chip in range(peers // 2):
        start = pl.multiple_of((2 * chip + mate) * features, features)
        bundle_ref[chip * rows : (chip + 1) * rows] = own_ref[2 * chip + mate]
        bundle_ref[2 * rows + chip * features : 2 * rows + (chip + 1) * features] = w_out_ref[pl.ds(start, features), :]


def project_query(tokens, weights, w_out, peers):
    rows, channels = tokens.shape[0], weights.shape[2] // peers
    return pl.pallas_call(
        project_query_kernel,
        in_specs=[VMEM] * 3,
        out_specs=[VMEM] * 2,
        out_shape=[
            jax.ShapeDtypeStruct((peers, rows, channels), jnp.bfloat16),
            jax.ShapeDtypeStruct((2 * rows + w_out.shape[0] // 2, channels), jnp.bfloat16),
        ],
        compiler_params=PARAMS,
        name="project_query",
    )(tokens, weights, w_out)


def pack_kernel(parts_ref, taps_ref, out_ref, flat_ref, packed_ref):
    peers, kinds, _, channels = parts_ref.shape
    half, chunk = channels // 2, 2 * kinds + 2
    for kind in range(kinds + 1):
        if kind < kinds:
            total = decode(parts_ref[0, kind])
            for peer in range(1, peers):
                total = total + decode(parts_ref[peer, kind])
            flat_ref[...] = total.T
        else:
            flat_ref[...] = taps_ref[...] * TAP_SCALE
        for j in range(2):
            packed_ref[pl.ds(2 * kind + j, half, stride=chunk), :] = flat_ref[pl.ds(j, half, stride=2), :]
    out_ref[...] = encode(packed_ref[...])


def pack(parts, taps):
    channels, rows = taps.shape
    kinds = parts.shape[1] + 1
    return pl.pallas_call(
        pack_kernel,
        in_specs=[VMEM, VMEM],
        out_specs=VMEM,
        out_shape=jax.ShapeDtypeStruct((kinds * channels, rows), jnp.bfloat16),
        scratch_shapes=[
            pltpu.VMEM((channels, rows), jnp.float32),
            pltpu.VMEM((kinds * channels, rows), jnp.float32),
        ],
        compiler_params=PARAMS,
        name="pack",
    )(parts, taps)


def split(values):
    high = values.astype(jnp.bfloat16)
    return high, (values - high.astype(jnp.float32)).astype(jnp.bfloat16)


def dot_right(values, table):
    high, low = split(values)
    return jnp.dot(jnp.concatenate([high, low, high], axis=1), table, preferred_element_type=jnp.float32)


def dot_left(table, values):
    high, low = split(values)
    return jnp.dot(table, jnp.concatenate([high, high, low], axis=0), preferred_element_type=jnp.float32)


def delayed(block, by):
    rows, cols = block.shape
    moved = pltpu.roll(block, by, 1)
    col = lax.broadcasted_iota(jnp.int32, (rows, cols), 1)
    row = lax.broadcasted_iota(jnp.int32, (rows, cols), 0)
    carried = jnp.where(row == 0, 0.0, pltpu.roll(moved, 1, 0))
    return jnp.where(col < by, carried, moved)


def convolve_kernel(turn, code_ref, short_ref, skip_ref, first_ref, twist_ref, mid_ref, inv_ref, last_ref, out_ref, now_ref, mix_ref):
    rows, cols = twist_ref.shape[1:]
    now_ref[...] = decode(code_ref[...])
    pair = lax.rem(lax.axis_index("seq") + rows - turn, rows)
    shift = short_ref.shape[2] - 2 * pair
    short = [pltpu.roll(short_ref[tap], shift, 1) for tap in range(3)]
    skip = pltpu.roll(skip_ref[...], shift, 1)

    def turned_back(row):
        return jnp.roll(now_ref[pl.ds(row, rows, stride=6), :], turn, axis=0)

    def mixed(kind, j):
        block = turned_back(2 * kind + j) * (1.0 / PROJ_SCALE)
        weights = [short[tap][kind + 1 : kind + 2, j : j + 1] for tap in range(3)]
        return weights[0] * block + weights[1] * delayed(block, 1) + weights[2] * delayed(block, 2)

    signal = [mixed(0, j) * mixed(1, j) for j in range(2)]
    taps = [turned_back(4 + j) * (1.0 / TAP_SCALE) for j in range(2)]
    data = jnp.concatenate(signal + taps, axis=1)
    spread = dot_left(first_ref[...], data)
    t_re, t_im = twist_ref[0], twist_ref[1]
    turned = []
    for k in range(4):
        re = spread[:rows, k * cols : (k + 1) * cols]
        im = spread[rows:, k * cols : (k + 1) * cols]
        turned.append(jnp.concatenate([re * t_re - im * t_im, re * t_im + im * t_re], axis=1))
    freq = dot_right(jnp.concatenate(turned, axis=0), mid_ref[...])
    both = []
    for j in range(2):
        s_re, s_im = freq[j * rows : (j + 1) * rows, :cols], freq[j * rows : (j + 1) * rows, cols:]
        h_re, h_im = freq[(2 + j) * rows : (3 + j) * rows, :cols], freq[(2 + j) * rows : (3 + j) * rows, cols:]
        both.append(jnp.concatenate([s_re * h_re - s_im * h_im, s_re * h_im + s_im * h_re], axis=1))
    back = dot_right(jnp.concatenate(both, axis=0), inv_ref[...])
    real, imag = [], []
    for j in range(2):
        re, im = back[j * rows : (j + 1) * rows, :cols], back[j * rows : (j + 1) * rows, cols:]
        real.append(re * t_re + im * t_im)
        imag.append(im * t_re - re * t_im)
    stacked = jnp.concatenate([jnp.concatenate(real, axis=1), jnp.concatenate(imag, axis=1)], axis=0)
    convolved = dot_left(last_ref[...], stacked)
    for j in range(2):
        outcome = convolved[:, j * cols : (j + 1) * cols] + skip[:, j : j + 1] * signal[j]
        mix_ref[pl.ds(j, rows, stride=2), :] = jnp.roll(outcome, -turn, axis=0)
    out_ref[...] = (mix_ref[...] * jnp.abs(mix_ref[...])).astype(jnp.bfloat16)


def tables(rows, cols):
    total = rows * cols
    a, b = np.arange(rows), np.arange(cols)
    first = np.exp(-2j * np.pi * np.outer(a, a) / rows - 0.5j * np.pi * a[None, :] / rows)
    twist = np.exp(-2j * np.pi * np.outer(a, b) / total - 0.5j * np.pi * b[None, :] / total)
    second = np.exp(-2j * np.pi * np.outer(b, b) / cols)

    def halves(table):
        table = table.astype(np.float32)
        high = table.astype(jnp.bfloat16)
        return high, (table - high.astype(np.float32)).astype(jnp.bfloat16)

    def at_left(table):
        high, low = halves(table)
        return jnp.asarray(np.concatenate([high, low, high], axis=1))

    def at_right(table):
        high, low = halves(table)
        return jnp.asarray(np.concatenate([high, high, low], axis=0))

    return (
        at_left(np.concatenate([first.real, first.imag])),
        jnp.asarray(np.stack([twist.real, twist.imag]).astype(np.float32)),
        at_right(np.block([[second.real, second.imag], [-second.imag, second.real]])),
        at_right(np.block([[second.real, -second.imag], [second.imag, second.real]])),
        at_left(np.concatenate([first.real.T, first.imag.T], axis=1) / total),
    )


def convolve(code, short, skip, rows, cols, turn):
    return pl.pallas_call(
        functools.partial(convolve_kernel, turn),
        in_specs=[VMEM] * 8,
        out_specs=VMEM,
        out_shape=jax.ShapeDtypeStruct((2 * rows, cols), jnp.bfloat16),
        scratch_shapes=[pltpu.VMEM((6 * rows, cols), jnp.float32), pltpu.VMEM((2 * rows, cols), jnp.float32)],
        compiler_params=PARAMS,
        name="convolve",
    )(code, short, skip, *tables(rows, cols))


def pair_query_kernel(own_ref, from_mate_ref, keep_ref, send_ref):
    index = lax.axis_index("fsdp")
    rows = keep_ref.shape[0]

    def total(peer):
        start = pl.multiple_of(lax.div(peer, 2) * rows, rows)
        return decode(own_ref[peer]) + decode(from_mate_ref[pl.ds(start, rows), :])

    keep_ref[...] = total(index)
    send_ref[...] = encode(total(index ^ 2))


def pair_query(own, from_mate):
    _, rows, channels = own.shape
    return pl.pallas_call(
        pair_query_kernel,
        in_specs=[VMEM, VMEM],
        out_specs=[VMEM, VMEM],
        out_shape=[
            jax.ShapeDtypeStruct((rows, channels), jnp.float32),
            jax.ShapeDtypeStruct((rows, channels), jnp.bfloat16),
        ],
        compiler_params=PARAMS,
        name="pair_query",
    )(own, from_mate)


def sum_query_kernel(keep_ref, code_ref, w_out_ref, from_mate_ref, out_ref, edge_ref, far_ref):
    rows, features = out_ref.shape[0], far_ref.shape[0] // 2
    index = lax.axis_index("fsdp")
    out_ref[...] = (keep_ref[...] + decode(code_ref[...])) * (1.0 / PROJ_SCALE)
    edge_ref[...] = out_ref[rows - 8 :]
    start = pl.multiple_of((index ^ 2) * features, features)
    far_ref[:features] = w_out_ref[pl.ds(start, features), :]
    start = pl.multiple_of(2 * rows + (1 - lax.div(index, 2)) * features, features)
    far_ref[features:] = from_mate_ref[pl.ds(start, features), :]


def sum_query(keep, code, w_out, from_mate):
    rows, channels = keep.shape
    return pl.pallas_call(
        sum_query_kernel,
        in_specs=[VMEM] * 4,
        out_specs=[VMEM] * 3,
        out_shape=[
            jax.ShapeDtypeStruct((rows, channels), jnp.float32),
            jax.ShapeDtypeStruct((8, channels), jnp.float32),
            jax.ShapeDtypeStruct((w_out.shape[0] // 2, channels), jnp.bfloat16),
        ],
        compiler_params=PARAMS,
        name="sum_query",
    )(keep, code, w_out, from_mate)


def mix_query_kernel(edge_ref, query_ref, short_ref, out_ref):
    rows = query_ref.shape[0]
    wide = jnp.concatenate([edge_ref[...], query_ref[...]], axis=0)
    total = short_ref[0, 0:1] * query_ref[...]
    for tap in range(1, 3):
        total = total + short_ref[tap, 0:1] * pltpu.roll(wide, tap, 0)[8 : 8 + rows]
    out_ref[...] = total.T


def mix_query(edge, query, short):
    return pl.pallas_call(
        mix_query_kernel,
        in_specs=[VMEM] * 3,
        out_specs=VMEM,
        out_shape=jax.ShapeDtypeStruct(query.shape[::-1], jnp.float32),
        compiler_params=PARAMS,
        name="mix_query",
    )(edge, query, short)


def gate_kernel(code_ref, query_ref, out_ref):
    wide = code_ref[...].astype(jnp.float32)
    out_ref[...] = (query_ref[...] * (wide * lax.rsqrt(jnp.maximum(jnp.abs(wide), TINY)))).astype(jnp.bfloat16)


def gate(code, query):
    return pl.pallas_call(
        gate_kernel,
        in_specs=[VMEM] * 2,
        out_specs=VMEM,
        out_shape=jax.ShapeDtypeStruct(query.shape, jnp.bfloat16),
        compiler_params=PARAMS,
        name="gate",
    )(code, query)


def output_kernel(gated_ref, w_out_ref, from_mate_ref, far_ref, out_ref):
    index = lax.axis_index("fsdp")
    rows, features = out_ref.shape
    channels = gated_ref.shape[0] // 4
    own = pl.multiple_of(index * features, features)
    mate = pl.multiple_of(2 * rows + lax.div(index, 2) * features, features)
    columns = [
        w_out_ref[pl.ds(own, features), :],
        from_mate_ref[pl.ds(mate, features), :],
        far_ref[:features],
        far_ref[features:],
    ]
    total = 0.0
    for step, column in enumerate(columns):
        start = pl.multiple_of((index ^ step) * channels, channels)
        total = total + jnp.dot(column, gated_ref[pl.ds(start, channels), :], preferred_element_type=jnp.float32)
    out_ref[...] = total.T


def output(gated, w_out, from_mate, far):
    return pl.pallas_call(
        output_kernel,
        in_specs=[VMEM] * 4,
        out_specs=VMEM,
        out_shape=jax.ShapeDtypeStruct((gated.shape[1], far.shape[0] // 2), jnp.float32),
        compiler_params=PARAMS,
        name="output",
    )(gated, w_out, from_mate, far)


def exchanged(piece, axis, step):
    return lax.ppermute(piece, axis, [(i, i ^ step) for i in range(lax.axis_size(axis))])


def on_device(tokens, w_in, short_w, long_filter, skip_gain, w_out):
    seq_count = lax.axis_size("seq")
    fsdp_count = lax.axis_size("fsdp")
    channels, local_tok = long_filter.shape
    turn = 88
    group = [[(i + turn) % seq_count for i in range(seq_count)]]
    weights = w_in.transpose(1, 0, 2)
    partial = project(tokens, weights, 1, 2, fsdp_count)
    parts = lax.all_to_all(partial, "fsdp", 0, 0, tiled=True)
    parts, tokens, w_out = lax.optimization_barrier((parts, tokens, w_out))
    query_parts, bundle = project_query(tokens, weights, w_out, fsdp_count)
    from_mate = exchanged(bundle, "fsdp", 1)
    keep, send = pair_query(query_parts, from_mate)
    other_chip = exchanged(send, "fsdp", 2)
    packed = pack(parts, long_filter).reshape(seq_count, 3, 2, local_tok).transpose(0, 2, 1, 3)
    whole = lax.all_to_all(packed.reshape(seq_count, 2, -1), "seq", 0, 0, tiled=True, axis_index_groups=group)
    whole = whole.reshape(seq_count, 2, 3, local_tok).transpose(0, 2, 1, 3).reshape(-1, local_tok)
    coded = convolve(whole, short_w, skip_gain.reshape(1, -1), seq_count, local_tok, turn)
    coded, other_chip, from_mate = lax.optimization_barrier((coded, other_chip, from_mate))
    query, edge, far = sum_query(keep, other_chip, w_out, from_mate)
    edge = lax.ppermute(edge, "seq", [(i, i + 1) for i in range(seq_count - 1)])
    query = mix_query(edge, query, short_w)
    far = exchanged(far, "fsdp", 2)
    home = lax.all_to_all(coded.reshape(seq_count, 2, local_tok), "seq", 0, 0, tiled=True, axis_index_groups=group)
    gated = gate(home.reshape(channels, local_tok), query)
    gathered = lax.all_gather(gated, "fsdp", axis=0, tiled=True)
    return output(gathered, w_out, from_mate, far)


def solution(mesh):
    in_specs = (
        P("seq", "fsdp"),
        P("fsdp", None, None),
        P(None, None, "fsdp"),
        P("fsdp", "seq"),
        P("fsdp"),
        P(None, "fsdp"),
    )
    out_specs = P("seq", "fsdp")
    return jax.shard_map(
        on_device, mesh=mesh, in_specs=in_specs, out_specs=out_specs, check_vma=False
    )
```

```python
import functools

import jax
import jax.numpy as jnp
import numpy as np
from jax import lax
from jax.experimental import pallas as pl
from jax.experimental.pallas import tpu as pltpu
from jax.sharding import PartitionSpec as P

PROJ_SCALE = 2.0**21
TAP_SCALE = 2.0**31
TINY = 1e-37
VMEM = pl.BlockSpec(memory_space=pltpu.VMEM)
SMEM = pl.BlockSpec(memory_space=pltpu.SMEM)
PARAMS = pltpu.CompilerParams(vmem_limit_bytes=32 * 1024 * 1024)


def encode(scaled):
    return ((scaled * scaled) * (scaled * jnp.abs(scaled))).astype(jnp.bfloat16)


def decode(code):
    wide = code.astype(jnp.float32)
    root = lax.rsqrt(lax.rsqrt(jnp.maximum(jnp.abs(wide), TINY)))
    return jnp.where(wide < 0, -root, root)


def project_kernel(first, tokens_hbm, w_hbm, out_ref, tokens_ref, w_ref, sems):
    peers, kinds, _, channels = out_ref.shape
    parts = (sems.shape[0] - 1) // kinds
    depth = w_ref.shape[1] // parts

    def piece(kind, part):
        cut = pl.ds(part * depth, depth)
        return pltpu.make_async_copy(w_hbm.at[first + kind, cut], w_ref.at[kind, cut], sems.at[kind * parts + part])

    tokens_copy = pltpu.make_async_copy(tokens_hbm, tokens_ref, sems.at[kinds * parts])
    tokens_copy.start()
    for kind in range(kinds):
        for part in range(parts):
            piece(kind, part).start()
    tokens_copy.wait()
    scaled = tokens_ref[...] * jnp.bfloat16(PROJ_SCALE)
    for kind in range(kinds):
        for part in range(parts):
            piece(kind, part).wait()
        for peer in range(peers):
            columns = w_ref[kind, :, peer * channels : (peer + 1) * channels]
            out_ref[peer, kind] = encode(jnp.dot(scaled, columns, preferred_element_type=jnp.float32))


def project(tokens, weights, first, kinds, peers):
    _, depth, wide = weights.shape
    rows, channels = tokens.shape[0], wide // peers
    return pl.pallas_call(
        functools.partial(project_kernel, first),
        in_specs=[pl.BlockSpec(memory_space=pltpu.HBM)] * 2,
        out_specs=VMEM,
        out_shape=jax.ShapeDtypeStruct((peers, kinds, rows, channels), jnp.bfloat16),
        scratch_shapes=[
            pltpu.VMEM(tokens.shape, tokens.dtype),
            pltpu.VMEM((kinds, depth, wide), weights.dtype),
            pltpu.SemaphoreType.DMA((kinds + 1,)),
        ],
        compiler_params=PARAMS,
        name="project",
    )(pltpu.with_memory_space_constraint(tokens, pltpu.HBM), pltpu.with_memory_space_constraint(weights, pltpu.HBM))


def project_query_kernel(tokens_ref, w_ref, w_out_ref, own_ref, bundle_ref):
    peers, rows, channels = own_ref.shape
    features = w_out_ref.shape[0] // peers
    mate = 1 - lax.rem(lax.axis_index("fsdp"), 2)
    scaled = tokens_ref[...] * jnp.bfloat16(PROJ_SCALE)
    for peer in range(peers):
        columns = w_ref[0, :, peer * channels : (peer + 1) * channels]
        own_ref[peer] = encode(jnp.dot(scaled, columns, preferred_element_type=jnp.float32))
    for chip in range(peers // 2):
        start = pl.multiple_of((2 * chip + mate) * features, features)
        bundle_ref[chip * rows : (chip + 1) * rows] = own_ref[2 * chip + mate]
        bundle_ref[2 * rows + chip * features : 2 * rows + (chip + 1) * features] = w_out_ref[pl.ds(start, features), :]


def project_query(tokens, weights, w_out, peers):
    rows, channels = tokens.shape[0], weights.shape[2] // peers
    return pl.pallas_call(
        project_query_kernel,
        in_specs=[VMEM] * 3,
        out_specs=[VMEM] * 2,
        out_shape=[
            jax.ShapeDtypeStruct((peers, rows, channels), jnp.bfloat16),
            jax.ShapeDtypeStruct((2 * rows + w_out.shape[0] // 2, channels), jnp.bfloat16),
        ],
        compiler_params=PARAMS,
        name="project_query",
    )(tokens, weights, w_out)


def pack_kernel(parts_ref, taps_ref, out_ref, flat_ref, packed_ref):
    peers, kinds, _, channels = parts_ref.shape
    half, chunk = channels // 2, 2 * kinds + 2
    for kind in range(kinds + 1):
        if kind < kinds:
            total = decode(parts_ref[0, kind])
            for peer in range(1, peers):
                total = total + decode(parts_ref[peer, kind])
            flat_ref[...] = total.T
        else:
            flat_ref[...] = taps_ref[...] * TAP_SCALE
        for j in range(2):
            packed_ref[pl.ds(2 * kind + j, half, stride=chunk), :] = flat_ref[pl.ds(j, half, stride=2), :]
    out_ref[...] = encode(packed_ref[...])


def pack(parts, taps):
    channels, rows = taps.shape
    kinds = parts.shape[1] + 1
    return pl.pallas_call(
        pack_kernel,
        in_specs=[VMEM, VMEM],
        out_specs=VMEM,
        out_shape=jax.ShapeDtypeStruct((kinds * channels, rows), jnp.bfloat16),
        scratch_shapes=[
            pltpu.VMEM((channels, rows), jnp.float32),
            pltpu.VMEM((kinds * channels, rows), jnp.float32),
        ],
        compiler_params=PARAMS,
        name="pack",
    )(parts, taps)


ALONG_X = 4
FIRST = (2, 12, 1)


def group_order(devices):
    along_z = devices // (2 * ALONG_X)
    return [
        (x + FIRST[0]) % ALONG_X * (2 * along_z) + (z + FIRST[1]) % along_z * 2 + (y + FIRST[2]) % 2
        for z in range(along_z)
        for x in range(ALONG_X)
        for y in range(2)
    ]


def group_place(device, devices):
    along_z = devices // (2 * ALONG_X)
    x = lax.rem(lax.div(device, 2 * along_z) + ALONG_X - FIRST[0], ALONG_X)
    z = lax.rem(lax.rem(lax.div(device, 2), along_z) + along_z - FIRST[1], along_z)
    y = lax.rem(device + 2 - FIRST[2], 2)
    return (z * ALONG_X + x) * 2 + y


def split(values):
    high = values.astype(jnp.bfloat16)
    return high, (values - high.astype(jnp.float32)).astype(jnp.bfloat16)


def dot_right(values, table):
    high, low = split(values)
    return jnp.dot(jnp.concatenate([high, low, high], axis=1), table, preferred_element_type=jnp.float32)


def dot_left(table, values):
    high, low = split(values)
    return jnp.dot(table, jnp.concatenate([high, high, low], axis=0), preferred_element_type=jnp.float32)


def delayed(block, by):
    rows, cols = block.shape
    moved = pltpu.roll(block, by, 1)
    col = lax.broadcasted_iota(jnp.int32, (rows, cols), 1)
    row = lax.broadcasted_iota(jnp.int32, (rows, cols), 0)
    carried = jnp.where(row == 0, 0.0, pltpu.roll(moved, 1, 0))
    return jnp.where(col < by, carried, moved)


def convolve_kernel(code_ref, order_ref, short_ref, skip_ref, first_ref, twist_ref, mid_ref, inv_ref, last_ref, out_ref, now_ref, mix_ref):
    rows, cols = twist_ref.shape[1:]
    now_ref[...] = code_ref[...].astype(jnp.float32)
    shift = short_ref.shape[2] - 2 * group_place(lax.axis_index("seq"), rows)
    short = [pltpu.roll(short_ref[tap], shift, 1) for tap in range(3)]
    skip = pltpu.roll(skip_ref[...], shift, 1)

    def in_order(row):
        code = now_ref[pl.ds(row, rows, stride=6), :].astype(jnp.bfloat16)
        return decode(jnp.dot(order_ref[0], code, preferred_element_type=jnp.float32))

    def mixed(kind, j):
        block = in_order(2 * kind + j) * (1.0 / PROJ_SCALE)
        weights = [short[tap][kind + 1 : kind + 2, j : j + 1] for tap in range(3)]
        return weights[0] * block + weights[1] * delayed(block, 1) + weights[2] * delayed(block, 2)

    signal = [mixed(0, j) * mixed(1, j) for j in range(2)]
    taps = [in_order(4 + j) * (1.0 / TAP_SCALE) for j in range(2)]
    data = jnp.concatenate(signal + taps, axis=1)
    spread = dot_left(first_ref[...], data)
    t_re, t_im = twist_ref[0], twist_ref[1]
    turned = []
    for k in range(4):
        re = spread[:rows, k * cols : (k + 1) * cols]
        im = spread[rows:, k * cols : (k + 1) * cols]
        turned.append(jnp.concatenate([re * t_re - im * t_im, re * t_im + im * t_re], axis=1))
    freq = dot_right(jnp.concatenate(turned, axis=0), mid_ref[...])
    both = []
    for j in range(2):
        s_re, s_im = freq[j * rows : (j + 1) * rows, :cols], freq[j * rows : (j + 1) * rows, cols:]
        h_re, h_im = freq[(2 + j) * rows : (3 + j) * rows, :cols], freq[(2 + j) * rows : (3 + j) * rows, cols:]
        both.append(jnp.concatenate([s_re * h_re - s_im * h_im, s_re * h_im + s_im * h_re], axis=1))
    back = dot_right(jnp.concatenate(both, axis=0), inv_ref[...])
    real, imag = [], []
    for j in range(2):
        re, im = back[j * rows : (j + 1) * rows, :cols], back[j * rows : (j + 1) * rows, cols:]
        real.append(re * t_re + im * t_im)
        imag.append(im * t_re - re * t_im)
    stacked = jnp.concatenate([jnp.concatenate(real, axis=1), jnp.concatenate(imag, axis=1)], axis=0)
    convolved = dot_left(last_ref[...], stacked)
    for j in range(2):
        outcome = convolved[:, j * cols : (j + 1) * cols] + skip[:, j : j + 1] * signal[j]
        code = (outcome * jnp.abs(outcome)).astype(jnp.bfloat16)
        code = jnp.dot(order_ref[1], code, preferred_element_type=jnp.float32)
        mix_ref[pl.ds(j, rows, stride=2), :] = code
    out_ref[...] = mix_ref[...].astype(jnp.bfloat16)


def tables(rows, cols):
    total = rows * cols
    a, b = np.arange(rows), np.arange(cols)
    first = np.exp(-2j * np.pi * np.outer(a, a) / rows - 0.5j * np.pi * a[None, :] / rows)
    twist = np.exp(-2j * np.pi * np.outer(a, b) / total - 0.5j * np.pi * b[None, :] / total)
    second = np.exp(-2j * np.pi * np.outer(b, b) / cols)

    def halves(table):
        table = table.astype(np.float32)
        high = table.astype(jnp.bfloat16)
        return high, (table - high.astype(np.float32)).astype(jnp.bfloat16)

    def at_left(table):
        high, low = halves(table)
        return jnp.asarray(np.concatenate([high, low, high], axis=1))

    def at_right(table):
        high, low = halves(table)
        return jnp.asarray(np.concatenate([high, high, low], axis=0))

    return (
        at_left(np.concatenate([first.real, first.imag])),
        jnp.asarray(np.stack([twist.real, twist.imag]).astype(np.float32)),
        at_right(np.block([[second.real, second.imag], [-second.imag, second.real]])),
        at_right(np.block([[second.real, -second.imag], [second.imag, second.real]])),
        at_left(np.concatenate([first.real.T, first.imag.T], axis=1) / total),
    )


def convolve(code, short, skip, rows, cols, order):
    place = np.argsort(order)
    order_table = jnp.asarray(np.stack([np.eye(rows)[place], np.eye(rows)[order]]), jnp.bfloat16)
    return pl.pallas_call(
        convolve_kernel,
        in_specs=[VMEM] * 9,
        out_specs=VMEM,
        out_shape=jax.ShapeDtypeStruct((2 * rows, cols), jnp.bfloat16),
        scratch_shapes=[pltpu.VMEM((6 * rows, cols), jnp.float32), pltpu.VMEM((2 * rows, cols), jnp.float32)],
        compiler_params=PARAMS,
        name="convolve",
    )(code, order_table, short, skip, *tables(rows, cols))


def pair_query_kernel(own_ref, from_mate_ref, keep_ref, send_ref):
    index = lax.axis_index("fsdp")
    rows = keep_ref.shape[0]

    def total(peer):
        start = pl.multiple_of(lax.div(peer, 2) * rows, rows)
        return decode(own_ref[peer]) + decode(from_mate_ref[pl.ds(start, rows), :])

    keep_ref[...] = total(index)
    send_ref[...] = encode(total(index ^ 2))


def pair_query(own, from_mate):
    _, rows, channels = own.shape
    return pl.pallas_call(
        pair_query_kernel,
        in_specs=[VMEM, VMEM],
        out_specs=[VMEM, VMEM],
        out_shape=[
            jax.ShapeDtypeStruct((rows, channels), jnp.float32),
            jax.ShapeDtypeStruct((rows, channels), jnp.bfloat16),
        ],
        compiler_params=PARAMS,
        name="pair_query",
    )(own, from_mate)


def sum_query_kernel(keep_ref, code_ref, w_out_ref, from_mate_ref, out_ref, edge_ref, far_ref):
    rows, features = out_ref.shape[0], far_ref.shape[0] // 2
    index = lax.axis_index("fsdp")
    out_ref[...] = (keep_ref[...] + decode(code_ref[...])) * (1.0 / PROJ_SCALE)
    edge_ref[...] = out_ref[rows - 8 :]
    start = pl.multiple_of((index ^ 2) * features, features)
    far_ref[:features] = w_out_ref[pl.ds(start, features), :]
    start = pl.multiple_of(2 * rows + (1 - lax.div(index, 2)) * features, features)
    far_ref[features:] = from_mate_ref[pl.ds(start, features), :]


def sum_query(keep, code, w_out, from_mate):
    rows, channels = keep.shape
    return pl.pallas_call(
        sum_query_kernel,
        in_specs=[VMEM] * 4,
        out_specs=[VMEM] * 3,
        out_shape=[
            jax.ShapeDtypeStruct((rows, channels), jnp.float32),
            jax.ShapeDtypeStruct((8, channels), jnp.float32),
            jax.ShapeDtypeStruct((w_out.shape[0] // 2, channels), jnp.bfloat16),
        ],
        compiler_params=PARAMS,
        name="sum_query",
    )(keep, code, w_out, from_mate)


def mix_query_kernel(edge_ref, query_ref, short_ref, out_ref):
    rows = query_ref.shape[0]
    wide = jnp.concatenate([edge_ref[...], query_ref[...]], axis=0)
    total = short_ref[0, 0:1] * query_ref[...]
    for tap in range(1, 3):
        total = total + short_ref[tap, 0:1] * pltpu.roll(wide, tap, 0)[8 : 8 + rows]
    out_ref[...] = total.T


def mix_query(edge, query, short):
    return pl.pallas_call(
        mix_query_kernel,
        in_specs=[VMEM] * 3,
        out_specs=VMEM,
        out_shape=jax.ShapeDtypeStruct(query.shape[::-1], jnp.float32),
        compiler_params=PARAMS,
        name="mix_query",
    )(edge, query, short)


def gate_kernel(code_ref, query_ref, out_ref):
    wide = code_ref[...].astype(jnp.float32)
    out_ref[...] = (query_ref[...] * (wide * lax.rsqrt(jnp.maximum(jnp.abs(wide), TINY)))).astype(jnp.bfloat16)


def gate(code, query):
    return pl.pallas_call(
        gate_kernel,
        in_specs=[VMEM] * 2,
        out_specs=VMEM,
        out_shape=jax.ShapeDtypeStruct(query.shape, jnp.bfloat16),
        compiler_params=PARAMS,
        name="gate",
    )(code, query)


def output_kernel(gated_ref, w_out_ref, from_mate_ref, far_ref, out_ref):
    index = lax.axis_index("fsdp")
    rows, features = out_ref.shape
    channels = gated_ref.shape[0] // 4
    own = pl.multiple_of(index * features, features)
    mate = pl.multiple_of(2 * rows + lax.div(index, 2) * features, features)
    columns = [
        w_out_ref[pl.ds(own, features), :],
        from_mate_ref[pl.ds(mate, features), :],
        far_ref[:features],
        far_ref[features:],
    ]
    total = 0.0
    for step, column in enumerate(columns):
        start = pl.multiple_of((index ^ step) * channels, channels)
        total = total + jnp.dot(column, gated_ref[pl.ds(start, channels), :], preferred_element_type=jnp.float32)
    out_ref[...] = total.T


def output(gated, w_out, from_mate, far):
    return pl.pallas_call(
        output_kernel,
        in_specs=[VMEM] * 4,
        out_specs=VMEM,
        out_shape=jax.ShapeDtypeStruct((gated.shape[1], far.shape[0] // 2), jnp.float32),
        compiler_params=PARAMS,
        name="output",
    )(gated, w_out, from_mate, far)


def exchanged(piece, axis, step):
    return lax.ppermute(piece, axis, [(i, i ^ step) for i in range(lax.axis_size(axis))])


def on_device(tokens, w_in, short_w, long_filter, skip_gain, w_out):
    seq_count = lax.axis_size("seq")
    fsdp_count = lax.axis_size("fsdp")
    channels, local_tok = long_filter.shape
    order = group_order(seq_count)
    group = [order]
    weights = w_in.transpose(1, 0, 2)
    partial = project(tokens, weights, 1, 2, fsdp_count)
    parts = lax.all_to_all(partial, "fsdp", 0, 0, tiled=True)
    parts, tokens, w_out = lax.optimization_barrier((parts, tokens, w_out))
    query_parts, bundle = project_query(tokens, weights, w_out, fsdp_count)
    from_mate = exchanged(bundle, "fsdp", 1)
    keep, send = pair_query(query_parts, from_mate)
    other_chip = exchanged(send, "fsdp", 2)
    packed = pack(parts, long_filter).reshape(seq_count, 3, 2, local_tok).transpose(0, 2, 1, 3)
    whole = lax.all_to_all(packed.reshape(seq_count, 2, -1), "seq", 0, 0, tiled=True, axis_index_groups=group)
    whole = whole.reshape(seq_count, 2, 3, local_tok).transpose(0, 2, 1, 3).reshape(-1, local_tok)
    coded = convolve(whole, short_w, skip_gain.reshape(1, -1), seq_count, local_tok, order)
    coded, other_chip, from_mate = lax.optimization_barrier((coded, other_chip, from_mate))
    query, edge, far = sum_query(keep, other_chip, w_out, from_mate)
    edge = lax.ppermute(edge, "seq", [(i, i + 1) for i in range(seq_count - 1)])
    query = mix_query(edge, query, short_w)
    far = exchanged(far, "fsdp", 2)
    home = lax.all_to_all(coded.reshape(seq_count, 2, local_tok), "seq", 0, 0, tiled=True, axis_index_groups=group)
    gated = gate(home.reshape(channels, local_tok), query)
    gathered = lax.all_gather(gated, "fsdp", axis=0, tiled=True)
    return output(gathered, w_out, from_mate, far)


def solution(mesh):
    in_specs = (
        P("seq", "fsdp"),
        P("fsdp", None, None),
        P(None, None, "fsdp"),
        P("fsdp", "seq"),
        P("fsdp"),
        P(None, "fsdp"),
    )
    out_specs = P("seq", "fsdp")
    return jax.shard_map(
        on_device, mesh=mesh, in_specs=in_specs, out_specs=out_specs, check_vma=False
    )
```

```python
import functools

import jax
import jax.numpy as jnp
import numpy as np
from jax import lax
from jax.experimental import pallas as pl
from jax.experimental.pallas import tpu as pltpu
from jax.sharding import PartitionSpec as P

PROJ_SCALE = 2.0**21
TAP_SCALE = 2.0**31
TINY = 1e-37
VMEM = pl.BlockSpec(memory_space=pltpu.VMEM)
SMEM = pl.BlockSpec(memory_space=pltpu.SMEM)
PARAMS = pltpu.CompilerParams(vmem_limit_bytes=32 * 1024 * 1024)


def encode(scaled):
    return ((scaled * scaled) * (scaled * jnp.abs(scaled))).astype(jnp.bfloat16)


def decode(code):
    wide = code.astype(jnp.float32)
    root = lax.rsqrt(lax.rsqrt(jnp.maximum(jnp.abs(wide), TINY)))
    return jnp.where(wide < 0, -root, root)


def project_kernel(first, tokens_hbm, w_hbm, out_ref, tokens_ref, w_ref, sems):
    peers, kinds, _, channels = out_ref.shape
    parts = (sems.shape[0] - 1) // kinds
    depth = w_ref.shape[1] // parts

    def piece(kind, part):
        cut = pl.ds(part * depth, depth)
        return pltpu.make_async_copy(w_hbm.at[first + kind, cut], w_ref.at[kind, cut], sems.at[kind * parts + part])

    tokens_copy = pltpu.make_async_copy(tokens_hbm, tokens_ref, sems.at[kinds * parts])
    tokens_copy.start()
    for kind in range(kinds):
        for part in range(parts):
            piece(kind, part).start()
    tokens_copy.wait()
    scaled = tokens_ref[...] * jnp.bfloat16(PROJ_SCALE)
    for kind in range(kinds):
        for part in range(parts):
            piece(kind, part).wait()
        for peer in range(peers):
            columns = w_ref[kind, :, peer * channels : (peer + 1) * channels]
            out_ref[peer, kind] = encode(jnp.dot(scaled, columns, preferred_element_type=jnp.float32))


def project(tokens, weights, first, kinds, peers):
    _, depth, wide = weights.shape
    rows, channels = tokens.shape[0], wide // peers
    return pl.pallas_call(
        functools.partial(project_kernel, first),
        in_specs=[pl.BlockSpec(memory_space=pltpu.HBM)] * 2,
        out_specs=VMEM,
        out_shape=jax.ShapeDtypeStruct((peers, kinds, rows, channels), jnp.bfloat16),
        scratch_shapes=[
            pltpu.VMEM(tokens.shape, tokens.dtype),
            pltpu.VMEM((kinds, depth, wide), weights.dtype),
            pltpu.SemaphoreType.DMA((kinds + 1,)),
        ],
        compiler_params=PARAMS,
        name="project",
    )(pltpu.with_memory_space_constraint(tokens, pltpu.HBM), pltpu.with_memory_space_constraint(weights, pltpu.HBM))


def project_query_kernel(tokens_ref, w_ref, w_out_ref, own_ref, bundle_ref):
    peers, rows, channels = own_ref.shape
    features = w_out_ref.shape[0] // peers
    mate = 1 - lax.rem(lax.axis_index("fsdp"), 2)
    scaled = tokens_ref[...] * jnp.bfloat16(PROJ_SCALE)
    for peer in range(peers):
        columns = w_ref[0, :, peer * channels : (peer + 1) * channels]
        own_ref[peer] = encode(jnp.dot(scaled, columns, preferred_element_type=jnp.float32))
    for chip in range(peers // 2):
        start = pl.multiple_of((2 * chip + mate) * features, features)
        bundle_ref[chip * rows : (chip + 1) * rows] = own_ref[2 * chip + mate]
        bundle_ref[2 * rows + chip * features : 2 * rows + (chip + 1) * features] = w_out_ref[pl.ds(start, features), :]


def project_query(tokens, weights, w_out, peers):
    rows, channels = tokens.shape[0], weights.shape[2] // peers
    return pl.pallas_call(
        project_query_kernel,
        in_specs=[VMEM] * 3,
        out_specs=[VMEM] * 2,
        out_shape=[
            jax.ShapeDtypeStruct((peers, rows, channels), jnp.bfloat16),
            jax.ShapeDtypeStruct((2 * rows + w_out.shape[0] // 2, channels), jnp.bfloat16),
        ],
        compiler_params=PARAMS,
        name="project_query",
    )(tokens, weights, w_out)


def pack_kernel(parts_ref, taps_ref, out_ref, flat_ref, packed_ref):
    peers, kinds, _, channels = parts_ref.shape
    half, chunk = channels // 2, 2 * kinds + 2
    for kind in range(kinds + 1):
        if kind < kinds:
            total = decode(parts_ref[0, kind])
            for peer in range(1, peers):
                total = total + decode(parts_ref[peer, kind])
            flat_ref[...] = total.T
        else:
            flat_ref[...] = taps_ref[...] * TAP_SCALE
        for j in range(2):
            packed_ref[pl.ds(2 * kind + j, half, stride=chunk), :] = flat_ref[pl.ds(j, half, stride=2), :]
    out_ref[...] = encode(packed_ref[...])


def pack(parts, taps):
    channels, rows = taps.shape
    kinds = parts.shape[1] + 1
    return pl.pallas_call(
        pack_kernel,
        in_specs=[VMEM, VMEM],
        out_specs=VMEM,
        out_shape=jax.ShapeDtypeStruct((kinds * channels, rows), jnp.bfloat16),
        scratch_shapes=[
            pltpu.VMEM((channels, rows), jnp.float32),
            pltpu.VMEM((kinds * channels, rows), jnp.float32),
        ],
        compiler_params=PARAMS,
        name="pack",
    )(parts, taps)


ALONG_X = 4
FIRST = (2, 12, 1)


def group_order(devices):
    along_z = devices // (2 * ALONG_X)
    return [
        (x + FIRST[0]) % ALONG_X * (2 * along_z) + (z + FIRST[1]) % along_z * 2 + (y + FIRST[2]) % 2
        for z in range(along_z)
        for x in range(ALONG_X)
        for y in range(2)
    ]


def group_place(device, devices):
    along_z = devices // (2 * ALONG_X)
    x = lax.rem(lax.div(device, 2 * along_z) + ALONG_X - FIRST[0], ALONG_X)
    z = lax.rem(lax.rem(lax.div(device, 2), along_z) + along_z - FIRST[1], along_z)
    y = lax.rem(device + 2 - FIRST[2], 2)
    return (z * ALONG_X + x) * 2 + y


def split(values):
    high = values.astype(jnp.bfloat16)
    return high, (values - high.astype(jnp.float32)).astype(jnp.bfloat16)


def dot_right(values, table):
    high, low = split(values)
    return jnp.dot(jnp.concatenate([high, low, high], axis=1), table, preferred_element_type=jnp.float32)


def dot_left(table, values):
    high, low = split(values)
    return jnp.dot(table, jnp.concatenate([high, high, low], axis=0), preferred_element_type=jnp.float32)


def delayed(block, by):
    rows, cols = block.shape
    moved = pltpu.roll(block, by, 1)
    col = lax.broadcasted_iota(jnp.int32, (rows, cols), 1)
    row = lax.broadcasted_iota(jnp.int32, (rows, cols), 0)
    carried = jnp.where(row == 0, 0.0, pltpu.roll(moved, 1, 0))
    return jnp.where(col < by, carried, moved)


def convolve_kernel(code_ref, order_ref, short_ref, skip_ref, first_ref, twist_ref, mid_ref, last_ref, out_ref, now_ref, mix_ref):
    rows, cols = twist_ref.shape[1:]
    now_ref[...] = code_ref[...].astype(jnp.float32)
    shift = short_ref.shape[2] - 2 * group_place(lax.axis_index("seq"), rows)
    short = [pltpu.roll(short_ref[tap], shift, 1) for tap in range(3)]
    skip = pltpu.roll(skip_ref[...], shift, 1)

    def in_order(row):
        code = now_ref[pl.ds(row, rows, stride=6), :].astype(jnp.bfloat16)
        return decode(jnp.dot(order_ref[0], code, preferred_element_type=jnp.float32))

    def mixed(kind, j):
        block = in_order(2 * kind + j) * (1.0 / PROJ_SCALE)
        weights = [short[tap][kind + 1 : kind + 2, j : j + 1] for tap in range(3)]
        return weights[0] * block + weights[1] * delayed(block, 1) + weights[2] * delayed(block, 2)

    signal = [mixed(0, j) * mixed(1, j) for j in range(2)]
    taps = [in_order(4 + j) * (1.0 / TAP_SCALE) for j in range(2)]
    data = jnp.concatenate(signal + taps, axis=1)
    spread = dot_left(first_ref[...], data)
    t_re, t_im = twist_ref[0], twist_ref[1]
    turned = []
    for k in range(4):
        re = spread[:rows, k * cols : (k + 1) * cols]
        im = spread[rows:, k * cols : (k + 1) * cols]
        turned.append(jnp.concatenate([re * t_re - im * t_im, re * t_im + im * t_re], axis=1))
    freq = dot_right(jnp.concatenate(turned, axis=0), mid_ref[...])
    both = []
    for j in range(2):
        s_re, s_im = freq[j * rows : (j + 1) * rows, :cols], freq[j * rows : (j + 1) * rows, cols:]
        h_re, h_im = freq[(2 + j) * rows : (3 + j) * rows, :cols], freq[(2 + j) * rows : (3 + j) * rows, cols:]
        both.append(jnp.concatenate([s_re * h_re - s_im * h_im, -s_re * h_im - s_im * h_re], axis=1))
    back = dot_right(jnp.concatenate(both, axis=0), mid_ref[...])
    real, imag = [], []
    for j in range(2):
        re, im = back[j * rows : (j + 1) * rows, :cols], back[j * rows : (j + 1) * rows, cols:]
        real.append(re * t_re - im * t_im)
        imag.append(-im * t_re - re * t_im)
    stacked = jnp.concatenate([jnp.concatenate(real, axis=1), jnp.concatenate(imag, axis=1)], axis=0)
    convolved = dot_left(last_ref[...], stacked)
    for j in range(2):
        outcome = convolved[:, j * cols : (j + 1) * cols] + skip[:, j : j + 1] * signal[j]
        code = (outcome * jnp.abs(outcome)).astype(jnp.bfloat16)
        code = jnp.dot(order_ref[1], code, preferred_element_type=jnp.float32)
        mix_ref[pl.ds(j, rows, stride=2), :] = code
    out_ref[...] = mix_ref[...].astype(jnp.bfloat16)


def tables(rows, cols):
    total = rows * cols
    a, b = np.arange(rows), np.arange(cols)
    first = np.exp(-2j * np.pi * np.outer(a, a) / rows - 0.5j * np.pi * a[None, :] / rows)
    twist = np.exp(-2j * np.pi * np.outer(a, b) / total - 0.5j * np.pi * b[None, :] / total)
    second = np.exp(-2j * np.pi * np.outer(b, b) / cols)

    def halves(table):
        table = table.astype(np.float32)
        high = table.astype(jnp.bfloat16)
        return high, (table - high.astype(np.float32)).astype(jnp.bfloat16)

    def at_left(table):
        high, low = halves(table)
        return jnp.asarray(np.concatenate([high, low, high], axis=1))

    def at_right(table):
        high, low = halves(table)
        return jnp.asarray(np.concatenate([high, high, low], axis=0))

    return (
        at_left(np.concatenate([first.real, first.imag])),
        jnp.asarray(np.stack([twist.real, twist.imag]).astype(np.float32)),
        at_right(np.block([[second.real, second.imag], [-second.imag, second.real]])),
        at_left(np.concatenate([first.real.T, first.imag.T], axis=1) / total),
    )


def convolve(code, short, skip, rows, cols, order):
    place = np.argsort(order)
    order_table = jnp.asarray(np.stack([np.eye(rows)[place], np.eye(rows)[order]]), jnp.bfloat16)
    return pl.pallas_call(
        convolve_kernel,
        in_specs=[VMEM] * 8,
        out_specs=VMEM,
        out_shape=jax.ShapeDtypeStruct((2 * rows, cols), jnp.bfloat16),
        scratch_shapes=[pltpu.VMEM((6 * rows, cols), jnp.float32), pltpu.VMEM((2 * rows, cols), jnp.float32)],
        compiler_params=PARAMS,
        name="convolve",
    )(code, order_table, short, skip, *tables(rows, cols))


def pair_query_kernel(own_ref, from_mate_ref, keep_ref, send_ref):
    index = lax.axis_index("fsdp")
    rows = keep_ref.shape[0]

    def total(peer):
        start = pl.multiple_of(lax.div(peer, 2) * rows, rows)
        return decode(own_ref[peer]) + decode(from_mate_ref[pl.ds(start, rows), :])

    keep_ref[...] = total(index)
    send_ref[...] = encode(total(index ^ 2))


def pair_query(own, from_mate):
    _, rows, channels = own.shape
    return pl.pallas_call(
        pair_query_kernel,
        in_specs=[VMEM, VMEM],
        out_specs=[VMEM, VMEM],
        out_shape=[
            jax.ShapeDtypeStruct((rows, channels), jnp.float32),
            jax.ShapeDtypeStruct((rows, channels), jnp.bfloat16),
        ],
        compiler_params=PARAMS,
        name="pair_query",
    )(own, from_mate)


def sum_query_kernel(keep_ref, code_ref, w_out_ref, from_mate_ref, out_ref, edge_ref, far_ref):
    rows, features = out_ref.shape[0], far_ref.shape[0] // 2
    index = lax.axis_index("fsdp")
    out_ref[...] = (keep_ref[...] + decode(code_ref[...])) * (1.0 / PROJ_SCALE)
    edge_ref[...] = out_ref[rows - 8 :]
    start = pl.multiple_of((index ^ 2) * features, features)
    far_ref[:features] = w_out_ref[pl.ds(start, features), :]
    start = pl.multiple_of(2 * rows + (1 - lax.div(index, 2)) * features, features)
    far_ref[features:] = from_mate_ref[pl.ds(start, features), :]


def sum_query(keep, code, w_out, from_mate):
    rows, channels = keep.shape
    return pl.pallas_call(
        sum_query_kernel,
        in_specs=[VMEM] * 4,
        out_specs=[VMEM] * 3,
        out_shape=[
            jax.ShapeDtypeStruct((rows, channels), jnp.float32),
            jax.ShapeDtypeStruct((8, channels), jnp.float32),
            jax.ShapeDtypeStruct((w_out.shape[0] // 2, channels), jnp.bfloat16),
        ],
        compiler_params=PARAMS,
        name="sum_query",
    )(keep, code, w_out, from_mate)


def mix_query_kernel(edge_ref, query_ref, short_ref, out_ref):
    rows = query_ref.shape[0]
    wide = jnp.concatenate([edge_ref[...], query_ref[...]], axis=0)
    total = short_ref[0, 0:1] * query_ref[...]
    for tap in range(1, 3):
        total = total + short_ref[tap, 0:1] * pltpu.roll(wide, tap, 0)[8 : 8 + rows]
    out_ref[...] = total.T


def mix_query(edge, query, short):
    return pl.pallas_call(
        mix_query_kernel,
        in_specs=[VMEM] * 3,
        out_specs=VMEM,
        out_shape=jax.ShapeDtypeStruct(query.shape[::-1], jnp.float32),
        compiler_params=PARAMS,
        name="mix_query",
    )(edge, query, short)


def gate_kernel(code_ref, query_ref, out_ref):
    wide = code_ref[...].astype(jnp.float32)
    out_ref[...] = (query_ref[...] * (wide * lax.rsqrt(jnp.maximum(jnp.abs(wide), TINY)))).astype(jnp.bfloat16)


def gate(code, query):
    return pl.pallas_call(
        gate_kernel,
        in_specs=[VMEM] * 2,
        out_specs=VMEM,
        out_shape=jax.ShapeDtypeStruct(query.shape, jnp.bfloat16),
        compiler_params=PARAMS,
        name="gate",
    )(code, query)


def output_kernel(gated_ref, w_out_ref, from_mate_ref, far_ref, out_ref):
    index = lax.axis_index("fsdp")
    rows, features = out_ref.shape
    channels = gated_ref.shape[0] // 4
    own = pl.multiple_of(index * features, features)
    mate = pl.multiple_of(2 * rows + lax.div(index, 2) * features, features)
    columns = [
        w_out_ref[pl.ds(own, features), :],
        from_mate_ref[pl.ds(mate, features), :],
        far_ref[:features],
        far_ref[features:],
    ]
    total = 0.0
    for step, column in enumerate(columns):
        start = pl.multiple_of((index ^ step) * channels, channels)
        total = total + jnp.dot(column, gated_ref[pl.ds(start, channels), :], preferred_element_type=jnp.float32)
    out_ref[...] = total.T


def output(gated, w_out, from_mate, far):
    return pl.pallas_call(
        output_kernel,
        in_specs=[VMEM] * 4,
        out_specs=VMEM,
        out_shape=jax.ShapeDtypeStruct((gated.shape[1], far.shape[0] // 2), jnp.float32),
        compiler_params=PARAMS,
        name="output",
    )(gated, w_out, from_mate, far)


def exchanged(piece, axis, step):
    return lax.ppermute(piece, axis, [(i, i ^ step) for i in range(lax.axis_size(axis))])


def on_device(tokens, w_in, short_w, long_filter, skip_gain, w_out):
    seq_count = lax.axis_size("seq")
    fsdp_count = lax.axis_size("fsdp")
    channels, local_tok = long_filter.shape
    order = group_order(seq_count)
    group = [order]
    weights = w_in.transpose(1, 0, 2)
    partial = project(tokens, weights, 1, 2, fsdp_count)
    parts = lax.all_to_all(partial, "fsdp", 0, 0, tiled=True)
    parts, tokens, w_out = lax.optimization_barrier((parts, tokens, w_out))
    query_parts, bundle = project_query(tokens, weights, w_out, fsdp_count)
    from_mate = exchanged(bundle, "fsdp", 1)
    keep, send = pair_query(query_parts, from_mate)
    other_chip = exchanged(send, "fsdp", 2)
    packed = pack(parts, long_filter).reshape(seq_count, 3, 2, local_tok).transpose(0, 2, 1, 3)
    whole = lax.all_to_all(packed.reshape(seq_count, 2, -1), "seq", 0, 0, tiled=True, axis_index_groups=group)
    whole = whole.reshape(seq_count, 2, 3, local_tok).transpose(0, 2, 1, 3).reshape(-1, local_tok)
    coded = convolve(whole, short_w, skip_gain.reshape(1, -1), seq_count, local_tok, order)
    coded, other_chip, from_mate = lax.optimization_barrier((coded, other_chip, from_mate))
    query, edge, far = sum_query(keep, other_chip, w_out, from_mate)
    edge = lax.ppermute(edge, "seq", [(i, i + 1) for i in range(seq_count - 1)])
    query = mix_query(edge, query, short_w)
    far = exchanged(far, "fsdp", 2)
    home = lax.all_to_all(coded.reshape(seq_count, 2, local_tok), "seq", 0, 0, tiled=True, axis_index_groups=group)
    gated = gate(home.reshape(channels, local_tok), query)
    gathered = lax.all_gather(gated, "fsdp", axis=0, tiled=True)
    return output(gathered, w_out, from_mate, far)


def solution(mesh):
    in_specs = (
        P("seq", "fsdp"),
        P("fsdp", None, None),
        P(None, None, "fsdp"),
        P("fsdp", "seq"),
        P("fsdp"),
        P(None, "fsdp"),
    )
    out_specs = P("seq", "fsdp")
    return jax.shard_map(
        on_device, mesh=mesh, in_specs=in_specs, out_specs=out_specs, check_vma=False
    )
```

```python
import functools

import jax
import jax.numpy as jnp
import numpy as np
from jax import lax
from jax.experimental import pallas as pl
from jax.experimental.pallas import tpu as pltpu
from jax.sharding import PartitionSpec as P

PROJ_SCALE = 2.0**21
TAP_SCALE = 2.0**31
TINY = 1e-37
VMEM = pl.BlockSpec(memory_space=pltpu.VMEM)
SMEM = pl.BlockSpec(memory_space=pltpu.SMEM)
PARAMS = pltpu.CompilerParams(vmem_limit_bytes=32 * 1024 * 1024)


def encode(scaled):
    return ((scaled * scaled) * (scaled * jnp.abs(scaled))).astype(jnp.bfloat16)


def decode(code):
    wide = code.astype(jnp.float32)
    root = lax.rsqrt(lax.rsqrt(jnp.maximum(jnp.abs(wide), TINY)))
    return jnp.where(wide < 0, -root, root)


def project_kernel(first, tokens_hbm, w_hbm, out_ref, tokens_ref, w_ref, sems):
    peers, kinds, _, channels = out_ref.shape
    parts = (sems.shape[0] - 1) // kinds
    depth = w_ref.shape[1] // parts

    def piece(kind, part):
        cut = pl.ds(part * depth, depth)
        return pltpu.make_async_copy(w_hbm.at[first + kind, cut], w_ref.at[kind, cut], sems.at[kind * parts + part])

    tokens_copy = pltpu.make_async_copy(tokens_hbm, tokens_ref, sems.at[kinds * parts])
    tokens_copy.start()
    for kind in range(kinds):
        for part in range(parts):
            piece(kind, part).start()
    tokens_copy.wait()
    scaled = tokens_ref[...] * jnp.bfloat16(PROJ_SCALE)
    for kind in range(kinds):
        for part in range(parts):
            piece(kind, part).wait()
        for peer in range(peers):
            columns = w_ref[kind, :, peer * channels : (peer + 1) * channels]
            out_ref[peer, kind] = encode(jnp.dot(scaled, columns, preferred_element_type=jnp.float32))


def project(tokens, weights, first, kinds, peers):
    _, depth, wide = weights.shape
    rows, channels = tokens.shape[0], wide // peers
    return pl.pallas_call(
        functools.partial(project_kernel, first),
        in_specs=[pl.BlockSpec(memory_space=pltpu.HBM)] * 2,
        out_specs=VMEM,
        out_shape=jax.ShapeDtypeStruct((peers, kinds, rows, channels), jnp.bfloat16),
        scratch_shapes=[
            pltpu.VMEM(tokens.shape, tokens.dtype),
            pltpu.VMEM((kinds, depth, wide), weights.dtype),
            pltpu.SemaphoreType.DMA((kinds + 1,)),
        ],
        compiler_params=PARAMS,
        name="project",
    )(pltpu.with_memory_space_constraint(tokens, pltpu.HBM), pltpu.with_memory_space_constraint(weights, pltpu.HBM))


def project_query_kernel(tokens_ref, w_ref, w_out_ref, own_ref, bundle_ref):
    peers, rows, channels = own_ref.shape
    features = w_out_ref.shape[0] // peers
    mate = 1 - lax.rem(lax.axis_index("fsdp"), 2)
    scaled = tokens_ref[...] * jnp.bfloat16(PROJ_SCALE)
    for peer in range(peers):
        columns = w_ref[0, :, peer * channels : (peer + 1) * channels]
        own_ref[peer] = encode(jnp.dot(scaled, columns, preferred_element_type=jnp.float32))
    for chip in range(peers // 2):
        start = pl.multiple_of((2 * chip + mate) * features, features)
        bundle_ref[chip * rows : (chip + 1) * rows] = own_ref[2 * chip + mate]
        bundle_ref[2 * rows + chip * features : 2 * rows + (chip + 1) * features] = w_out_ref[pl.ds(start, features), :]


def project_query(tokens, weights, w_out, peers):
    rows, channels = tokens.shape[0], weights.shape[2] // peers
    return pl.pallas_call(
        project_query_kernel,
        in_specs=[VMEM] * 3,
        out_specs=[VMEM] * 2,
        out_shape=[
            jax.ShapeDtypeStruct((peers, rows, channels), jnp.bfloat16),
            jax.ShapeDtypeStruct((2 * rows + w_out.shape[0] // 2, channels), jnp.bfloat16),
        ],
        compiler_params=PARAMS,
        name="project_query",
    )(tokens, weights, w_out)


def pack_kernel(parts_ref, taps_ref, out_ref, flat_ref, packed_ref):
    peers, kinds, _, channels = parts_ref.shape
    half, chunk = channels // 2, 2 * kinds + 2
    for kind in range(kinds + 1):
        if kind < kinds:
            total = decode(parts_ref[0, kind])
            for peer in range(1, peers):
                total = total + decode(parts_ref[peer, kind])
            flat_ref[...] = total.T
        else:
            flat_ref[...] = taps_ref[...] * TAP_SCALE
        for j in range(2):
            packed_ref[pl.ds(2 * kind + j, half, stride=chunk), :] = flat_ref[pl.ds(j, half, stride=2), :]
    out_ref[...] = encode(packed_ref[...])


def pack(parts, taps):
    channels, rows = taps.shape
    kinds = parts.shape[1] + 1
    return pl.pallas_call(
        pack_kernel,
        in_specs=[VMEM, VMEM],
        out_specs=VMEM,
        out_shape=jax.ShapeDtypeStruct((kinds * channels, rows), jnp.bfloat16),
        scratch_shapes=[
            pltpu.VMEM((channels, rows), jnp.float32),
            pltpu.VMEM((kinds * channels, rows), jnp.float32),
        ],
        compiler_params=PARAMS,
        name="pack",
    )(parts, taps)


ALONG_X = 4
FIRST = (2, 12, 1)


def group_order(devices):
    along_z = devices // (2 * ALONG_X)
    return [
        (x + FIRST[0]) % ALONG_X * (2 * along_z) + (z + FIRST[1]) % along_z * 2 + (y + FIRST[2]) % 2
        for z in range(along_z)
        for x in range(ALONG_X)
        for y in range(2)
    ]


def group_place(device, devices):
    along_z = devices // (2 * ALONG_X)
    x = lax.rem(lax.div(device, 2 * along_z) + ALONG_X - FIRST[0], ALONG_X)
    z = lax.rem(lax.rem(lax.div(device, 2), along_z) + along_z - FIRST[1], along_z)
    y = lax.rem(device + 2 - FIRST[2], 2)
    return (z * ALONG_X + x) * 2 + y


def split(values):
    high = values.astype(jnp.bfloat16)
    return high, (values - high.astype(jnp.float32)).astype(jnp.bfloat16)


def dot_right(values, table):
    high, low = split(values)
    return jnp.dot(jnp.concatenate([high, low, high], axis=1), table, preferred_element_type=jnp.float32)


def dot_left(table, values):
    high, low = split(values)
    return jnp.dot(table, jnp.concatenate([high, high, low], axis=0), preferred_element_type=jnp.float32)


def delayed(block, by):
    rows, cols = block.shape
    moved = pltpu.roll(block, by, 1)
    col = lax.broadcasted_iota(jnp.int32, (rows, cols), 1)
    row = lax.broadcasted_iota(jnp.int32, (rows, cols), 0)
    carried = jnp.where(row == 0, 0.0, pltpu.roll(moved, 1, 0))
    return jnp.where(col < by, carried, moved)


def convolve_kernel(code_ref, order_ref, short_ref, skip_ref, first_ref, twist_ref, mid_ref, last_ref, out_ref, now_ref, mix_ref):
    rows, cols = twist_ref.shape[1:]
    now_ref[...] = code_ref[...].astype(jnp.float32)
    shift = short_ref.shape[2] - 2 * group_place(lax.axis_index("seq"), rows)
    short = [pltpu.roll(short_ref[tap], shift, 1) for tap in range(3)]
    skip = pltpu.roll(skip_ref[...], shift, 1)

    codes = [now_ref[pl.ds(row, rows, stride=6), :].astype(jnp.bfloat16) for row in range(6)]
    codes = jnp.dot(order_ref[0], jnp.concatenate(codes, axis=1), preferred_element_type=jnp.float32)

    def in_order(row):
        return decode(codes[:, row * cols : (row + 1) * cols])

    def mixed(kind, j):
        block = in_order(2 * kind + j) * (1.0 / PROJ_SCALE)
        weights = [short[tap][kind + 1 : kind + 2, j : j + 1] for tap in range(3)]
        return weights[0] * block + weights[1] * delayed(block, 1) + weights[2] * delayed(block, 2)

    signal = [mixed(0, j) * mixed(1, j) for j in range(2)]
    taps = [in_order(4 + j) * (1.0 / TAP_SCALE) for j in range(2)]
    data = jnp.concatenate(signal + taps, axis=1)
    spread = dot_left(first_ref[...], data)
    t_re, t_im = twist_ref[0], twist_ref[1]
    turned = []
    for k in range(4):
        re = spread[:rows, k * cols : (k + 1) * cols]
        im = spread[rows:, k * cols : (k + 1) * cols]
        turned.append(jnp.concatenate([re * t_re - im * t_im, re * t_im + im * t_re], axis=1))
    freq = dot_right(jnp.concatenate(turned, axis=0), mid_ref[...])
    both = []
    for j in range(2):
        s_re, s_im = freq[j * rows : (j + 1) * rows, :cols], freq[j * rows : (j + 1) * rows, cols:]
        h_re, h_im = freq[(2 + j) * rows : (3 + j) * rows, :cols], freq[(2 + j) * rows : (3 + j) * rows, cols:]
        both.append(jnp.concatenate([s_re * h_re - s_im * h_im, -s_re * h_im - s_im * h_re], axis=1))
    back = dot_right(jnp.concatenate(both, axis=0), mid_ref[...])
    real, imag = [], []
    for j in range(2):
        re, im = back[j * rows : (j + 1) * rows, :cols], back[j * rows : (j + 1) * rows, cols:]
        real.append(re * t_re - im * t_im)
        imag.append(-im * t_re - re * t_im)
    stacked = jnp.concatenate([jnp.concatenate(real, axis=1), jnp.concatenate(imag, axis=1)], axis=0)
    convolved = dot_left(last_ref[...], stacked)
    outcomes = [convolved[:, j * cols : (j + 1) * cols] + skip[:, j : j + 1] * signal[j] for j in range(2)]
    outcome = jnp.concatenate(outcomes, axis=1)
    code = (outcome * jnp.abs(outcome)).astype(jnp.bfloat16)
    code = jnp.dot(order_ref[1], code, preferred_element_type=jnp.float32)
    for j in range(2):
        mix_ref[pl.ds(j, rows, stride=2), :] = code[:, j * cols : (j + 1) * cols]
    out_ref[...] = mix_ref[...].astype(jnp.bfloat16)


def tables(rows, cols):
    total = rows * cols
    a, b = np.arange(rows), np.arange(cols)
    first = np.exp(-2j * np.pi * np.outer(a, a) / rows - 0.5j * np.pi * a[None, :] / rows)
    twist = np.exp(-2j * np.pi * np.outer(a, b) / total - 0.5j * np.pi * b[None, :] / total)
    second = np.exp(-2j * np.pi * np.outer(b, b) / cols)

    def halves(table):
        table = table.astype(np.float32)
        high = table.astype(jnp.bfloat16)
        return high, (table - high.astype(np.float32)).astype(jnp.bfloat16)

    def at_left(table):
        high, low = halves(table)
        return jnp.asarray(np.concatenate([high, low, high], axis=1))

    def at_right(table):
        high, low = halves(table)
        return jnp.asarray(np.concatenate([high, high, low], axis=0))

    return (
        at_left(np.concatenate([first.real, first.imag])),
        jnp.asarray(np.stack([twist.real, twist.imag]).astype(np.float32)),
        at_right(np.block([[second.real, second.imag], [-second.imag, second.real]])),
        at_left(np.concatenate([first.real.T, first.imag.T], axis=1) / total),
    )


def convolve(code, short, skip, rows, cols, order):
    place = np.argsort(order)
    order_table = jnp.asarray(np.stack([np.eye(rows)[place], np.eye(rows)[order]]), jnp.bfloat16)
    return pl.pallas_call(
        convolve_kernel,
        in_specs=[VMEM] * 8,
        out_specs=VMEM,
        out_shape=jax.ShapeDtypeStruct((2 * rows, cols), jnp.bfloat16),
        scratch_shapes=[pltpu.VMEM((6 * rows, cols), jnp.float32), pltpu.VMEM((2 * rows, cols), jnp.float32)],
        compiler_params=PARAMS,
        name="convolve",
    )(code, order_table, short, skip, *tables(rows, cols))


def pair_query_kernel(own_ref, from_mate_ref, keep_ref, send_ref):
    index = lax.axis_index("fsdp")
    rows = keep_ref.shape[0]

    def total(peer):
        start = pl.multiple_of(lax.div(peer, 2) * rows, rows)
        return decode(own_ref[peer]) + decode(from_mate_ref[pl.ds(start, rows), :])

    keep_ref[...] = total(index)
    send_ref[...] = encode(total(index ^ 2))


def pair_query(own, from_mate):
    _, rows, channels = own.shape
    return pl.pallas_call(
        pair_query_kernel,
        in_specs=[VMEM, VMEM],
        out_specs=[VMEM, VMEM],
        out_shape=[
            jax.ShapeDtypeStruct((rows, channels), jnp.float32),
            jax.ShapeDtypeStruct((rows, channels), jnp.bfloat16),
        ],
        compiler_params=PARAMS,
        name="pair_query",
    )(own, from_mate)


def sum_query_kernel(keep_ref, code_ref, w_out_ref, from_mate_ref, out_ref, edge_ref, far_ref):
    rows, features = out_ref.shape[0], far_ref.shape[0] // 2
    index = lax.axis_index("fsdp")
    out_ref[...] = (keep_ref[...] + decode(code_ref[...])) * (1.0 / PROJ_SCALE)
    edge_ref[...] = out_ref[rows - 8 :]
    start = pl.multiple_of((index ^ 2) * features, features)
    far_ref[:features] = w_out_ref[pl.ds(start, features), :]
    start = pl.multiple_of(2 * rows + (1 - lax.div(index, 2)) * features, features)
    far_ref[features:] = from_mate_ref[pl.ds(start, features), :]


def sum_query(keep, code, w_out, from_mate):
    rows, channels = keep.shape
    return pl.pallas_call(
        sum_query_kernel,
        in_specs=[VMEM] * 4,
        out_specs=[VMEM] * 3,
        out_shape=[
            jax.ShapeDtypeStruct((rows, channels), jnp.float32),
            jax.ShapeDtypeStruct((8, channels), jnp.float32),
            jax.ShapeDtypeStruct((w_out.shape[0] // 2, channels), jnp.bfloat16),
        ],
        compiler_params=PARAMS,
        name="sum_query",
    )(keep, code, w_out, from_mate)


def mix_query_kernel(edge_ref, query_ref, short_ref, out_ref):
    rows = query_ref.shape[0]
    wide = jnp.concatenate([edge_ref[...], query_ref[...]], axis=0)
    total = short_ref[0, 0:1] * query_ref[...]
    for tap in range(1, 3):
        total = total + short_ref[tap, 0:1] * pltpu.roll(wide, tap, 0)[8 : 8 + rows]
    out_ref[...] = total.T


def mix_query(edge, query, short):
    return pl.pallas_call(
        mix_query_kernel,
        in_specs=[VMEM] * 3,
        out_specs=VMEM,
        out_shape=jax.ShapeDtypeStruct(query.shape[::-1], jnp.float32),
        compiler_params=PARAMS,
        name="mix_query",
    )(edge, query, short)


def gate_kernel(code_ref, query_ref, out_ref):
    wide = code_ref[...].astype(jnp.float32)
    out_ref[...] = (query_ref[...] * (wide * lax.rsqrt(jnp.maximum(jnp.abs(wide), TINY)))).astype(jnp.bfloat16)


def gate(code, query):
    return pl.pallas_call(
        gate_kernel,
        in_specs=[VMEM] * 2,
        out_specs=VMEM,
        out_shape=jax.ShapeDtypeStruct(query.shape, jnp.bfloat16),
        compiler_params=PARAMS,
        name="gate",
    )(code, query)


def output_kernel(gated_ref, w_out_ref, from_mate_ref, far_ref, out_ref):
    index = lax.axis_index("fsdp")
    rows, features = out_ref.shape
    channels = gated_ref.shape[0] // 4
    own = pl.multiple_of(index * features, features)
    mate = pl.multiple_of(2 * rows + lax.div(index, 2) * features, features)
    columns = [
        w_out_ref[pl.ds(own, features), :],
        from_mate_ref[pl.ds(mate, features), :],
        far_ref[:features],
        far_ref[features:],
    ]
    total = 0.0
    for step, column in enumerate(columns):
        start = pl.multiple_of((index ^ step) * channels, channels)
        total = total + jnp.dot(column, gated_ref[pl.ds(start, channels), :], preferred_element_type=jnp.float32)
    out_ref[...] = total.T


def output(gated, w_out, from_mate, far):
    return pl.pallas_call(
        output_kernel,
        in_specs=[VMEM] * 4,
        out_specs=VMEM,
        out_shape=jax.ShapeDtypeStruct((gated.shape[1], far.shape[0] // 2), jnp.float32),
        compiler_params=PARAMS,
        name="output",
    )(gated, w_out, from_mate, far)


def exchanged(piece, axis, step):
    return lax.ppermute(piece, axis, [(i, i ^ step) for i in range(lax.axis_size(axis))])


def on_device(tokens, w_in, short_w, long_filter, skip_gain, w_out):
    seq_count = lax.axis_size("seq")
    fsdp_count = lax.axis_size("fsdp")
    channels, local_tok = long_filter.shape
    order = group_order(seq_count)
    group = [order]
    weights = w_in.transpose(1, 0, 2)
    partial = project(tokens, weights, 1, 2, fsdp_count)
    parts = lax.all_to_all(partial, "fsdp", 0, 0, tiled=True)
    parts, tokens, w_out = lax.optimization_barrier((parts, tokens, w_out))
    query_parts, bundle = project_query(tokens, weights, w_out, fsdp_count)
    from_mate = exchanged(bundle, "fsdp", 1)
    keep, send = pair_query(query_parts, from_mate)
    other_chip = exchanged(send, "fsdp", 2)
    packed = pack(parts, long_filter).reshape(seq_count, 3, 2, local_tok).transpose(0, 2, 1, 3)
    whole = lax.all_to_all(packed.reshape(seq_count, 2, -1), "seq", 0, 0, tiled=True, axis_index_groups=group)
    whole = whole.reshape(seq_count, 2, 3, local_tok).transpose(0, 2, 1, 3).reshape(-1, local_tok)
    coded = convolve(whole, short_w, skip_gain.reshape(1, -1), seq_count, local_tok, order)
    coded, other_chip, from_mate = lax.optimization_barrier((coded, other_chip, from_mate))
    query, edge, far = sum_query(keep, other_chip, w_out, from_mate)
    edge = lax.ppermute(edge, "seq", [(i, i + 1) for i in range(seq_count - 1)])
    query = mix_query(edge, query, short_w)
    far = exchanged(far, "fsdp", 2)
    home = lax.all_to_all(coded.reshape(seq_count, 2, local_tok), "seq", 0, 0, tiled=True, axis_index_groups=group)
    gated = gate(home.reshape(channels, local_tok), query)
    gathered = lax.all_gather(gated, "fsdp", axis=0, tiled=True)
    return output(gathered, w_out, from_mate, far)


def solution(mesh):
    in_specs = (
        P("seq", "fsdp"),
        P("fsdp", None, None),
        P(None, None, "fsdp"),
        P("fsdp", "seq"),
        P("fsdp"),
        P(None, "fsdp"),
    )
    out_specs = P("seq", "fsdp")
    return jax.shard_map(
        on_device, mesh=mesh, in_specs=in_specs, out_specs=out_specs, check_vma=False
    )
```
